128 devices in a mesh: section: 8 (over z, y_lo), expert: 16 (over y_hi, x, core).
Axes of the slice: x: 4, y: 4 (y_hi: 2, y_lo: 2; y = y_hi * 2 + y_lo), z: 4, core: 2. Of those that a mesh axis runs over, the one named last changes fastest.
Arguments:
- act_in: bfloat16 [8, 1024, 3584], P('section', 'expert'), may hold values from -6 to 6
- grad_in: bfloat16 [8, 1024, 3584], P('section', 'expert'), may hold values from -6 to 6
- feed: bfloat16 [1, 1024, 3584], P(None, 'expert'), may hold values from -6 to 6
- loss_grad: bfloat16 [1, 1024, 3584], P(None, 'expert'), may hold values from -6 to 6
- saved: bfloat16 [8, 2, 1024, 3584], P('section', None, 'expert'), may hold values from -6 to 6
- fwd_gain: float32 [8, 3584], P('section'), may hold values from 0.1 to 1.9
- fwd_router: bfloat16 [8, 3584, 8], P('section'), may hold values from -0.09375 to 0.09375
- fwd_gate: bfloat16 [8, 3584, 8192], P('section', None, 'expert'), may hold values from -0.09375 to 0.09375
- fwd_up: bfloat16 [8, 3584, 8192], P('section', None, 'expert'), may hold values from -0.09375 to 0.09375
- fwd_down: bfloat16 [8, 8192, 3584], P('section', 'expert'), may hold values from -0.1875 to 0.1875
- bwd_gain: float32 [8, 3584], P('section'), may hold values from 0.1 to 1.9
- bwd_router: bfloat16 [8, 3584, 8], P('section'), may hold values from -0.09375 to 0.09375
- bwd_gate: bfloat16 [8, 3584, 8192], P('section', None, 'expert'), may hold values from -0.09375 to 0.09375
- bwd_up: bfloat16 [8, 3584, 8192], P('section', None, 'expert'), may hold values from -0.09375 to 0.09375
- bwd_down: bfloat16 [8, 8192, 3584], P('section', 'expert'), may hold values from -0.1875 to 0.1875
- fwd_routes: int32 [8, 2, 1024, 2], P('section', None, 'expert'), may hold values from 0 to 7, as said below
- bwd_routes: int32 [8, 2, 1024, 2], P('section', None, 'expert'), may hold values from 0 to 7, as said below
Outputs:
- fwd_out: bfloat16 [8, 2, 1024, 3584], P('section', None, 'expert')
- bwd_out: bfloat16 [8, 2, 1024, 3584], P('section', None, 'expert')
The draws below stay inside these ranges and needn't reach their ends.
Inputs may be any that keep to these rules, and one draw needn't show every extreme that they name: `fwd_routes`: each row names 2 different experts. In the 64 rows of one device for one step no expert is named by more than 24 rows; in every step of every layer some expert is named by exactly 24 rows of every device. `bwd_routes`: as for fwd_routes.
All inputs are finite; a program needn't handle non-finite values.
Results may differ from the reference program's by a relative error of at most 0.02.
Values may be sent and summed in bfloat16 or wider, within the bound.
A program may use at most 128 MiB of HBM per device.

```python
import jax
import jax.numpy as jnp
from jax import lax

D = 3584
EXP_HID = 1024
TOPK = 2
TICKS = 2
ROWS = 64
EXPERTS = 8
MB = 1024
CAP = 24
N_SECTION = 8
N_EXPERT = 16


def route_block(key, hot_expert):
    rank_key, column_key, mapping_key, offset_key = jax.random.split(key, 4)
    row_rank = jax.random.permutation(rank_key, ROWS)
    hot_row = row_rank < CAP
    hot_column = jax.random.randint(column_key, (ROWS,), 0, TOPK)
    others = (hot_expert + 1 + jax.random.permutation(mapping_key, EXPERTS - 1)) % EXPERTS
    offset = jax.random.randint(offset_key, (), 0, EXPERTS - 1)
    used_slots = TOPK - hot_row.astype(jnp.int32)
    before = jnp.cumsum(used_slots) - used_slots
    column = jnp.arange(TOPK, dtype=jnp.int32)[None, :]
    shifted = jnp.where(hot_row[:, None] & (column > hot_column[:, None]), column - 1, column)
    cyclic = (offset + before[:, None] + shifted) % (EXPERTS - 1)
    picked = jnp.take(others, cyclic)
    return jnp.where(hot_row[:, None] & (column == hot_column[:, None]), hot_expert, picked).astype(jnp.int32)


def route_table(key):
    hot_key, block_key = jax.random.split(key)
    hot_table = jax.random.randint(hot_key, (N_SECTION * TICKS,), 0, EXPERTS)
    hot_list = jnp.repeat(hot_table, N_EXPERT)
    block_keys = jax.random.split(block_key, N_SECTION * TICKS * N_EXPERT)
    blocks = jax.vmap(route_block)(block_keys, hot_list)
    return blocks.reshape(N_SECTION, TICKS, N_EXPERT * ROWS, TOPK).astype(jnp.int32)


def draw_fwd_routes(key, part):
    key = jax.random.fold_in(key, 11)
    return route_table(key)


def draw_bwd_routes(key, part):
    key = jax.random.fold_in(key, 23)
    return route_table(key)


def level_of(stream_key, shape, pieces, low, high):
    gain = 1.0
    for position, parts in pieces:
        steps = jax.random.uniform(jax.random.fold_in(jax.random.fold_in(stream_key, 6), position), (parts,), jnp.float32, low / len(pieces), high / len(pieces))
        gain = gain * jnp.repeat(jnp.exp(steps), shape[position] // parts).reshape((-1,) + (1,) * (len(shape) - 1 - position))
    return gain


def noise(own_key, dims, width, limit, pieces=(), kind=jnp.bfloat16):
    factor_of = level_of(own_key, dims, pieces, -0.22, 0.18) if pieces else 1.0
    drawn = jax.random.normal(own_key, dims, jnp.float32) * width * factor_of
    return jnp.minimum(jnp.maximum(drawn, -limit), limit).astype(kind)


def setup_inputs(seed: int = 0) -> dict:
    seeds = jax.random.split(jax.random.key(seed), 18)
    return {
        "act_in": noise(seeds[0], (N_SECTION, MB, D), 1.0, 6.0, ((0, 8), (1, 16))),
        "grad_in": noise(seeds[1], (N_SECTION, MB, D), 1.0, 6.0, ((0, 8), (1, 16))),
        "feed": noise(seeds[2], (TICKS - 1, MB, D), 1.0, 6.0, ((1, 16),)),
        "loss_grad": noise(seeds[3], (TICKS - 1, MB, D), 1.0, 6.0, ((1, 16),)),
        "saved": noise(seeds[4], (N_SECTION, TICKS, MB, D), 1.0, 6.0, ((0, 8), (2, 16))),
        "fwd_gain": jnp.clip(1.0 + 0.18 * jax.random.normal(seeds[5], (N_SECTION, D), jnp.float32), 0.1, 1.9),
        "fwd_router": noise(seeds[6], (N_SECTION, D, EXPERTS), D ** -0.5, 0.09375, ((0, 8),)),
        "fwd_gate": noise(seeds[7], (N_SECTION, D, EXPERTS * EXP_HID), D ** -0.5, 0.09375, ((0, 8), (2, 16))),
        "fwd_up": noise(seeds[8], (N_SECTION, D, EXPERTS * EXP_HID), D ** -0.5, 0.09375, ((0, 8), (2, 16))),
        "fwd_down": noise(seeds[9], (N_SECTION, EXPERTS * EXP_HID, D), EXP_HID ** -0.5, 0.1875, ((0, 8), (1, 16))),
        "bwd_gain": jnp.clip(1.0 + 0.18 * jax.random.normal(seeds[10], (N_SECTION, D), jnp.float32), 0.1, 1.9),
        "bwd_router": noise(seeds[11], (N_SECTION, D, EXPERTS), D ** -0.5, 0.09375, ((0, 8),)),
        "bwd_gate": noise(seeds[12], (N_SECTION, D, EXPERTS * EXP_HID), D ** -0.5, 0.09375, ((0, 8), (2, 16))),
        "bwd_up": noise(seeds[13], (N_SECTION, D, EXPERTS * EXP_HID), D ** -0.5, 0.09375, ((0, 8), (2, 16))),
        "bwd_down": noise(seeds[14], (N_SECTION, EXPERTS * EXP_HID, D), EXP_HID ** -0.5, 0.1875, ((0, 8), (1, 16))),
        "fwd_routes": draw_fwd_routes(jax.random.fold_in(seeds[17], 71), 0),
        "bwd_routes": draw_bwd_routes(jax.random.fold_in(seeds[17], 71), 0),
    }


NORM_EPS = 1e-06
ROUTE_SCALE = 2.5

def to_float(values):
    return values.astype(jnp.float32)

def normalize(inputs, norm_gain):
    widened = to_float(inputs)
    inv_rms = lax.rsqrt(lax.optimization_barrier(jnp.mean(widened * widened, axis=-1, keepdims=True)) + NORM_EPS)
    return ((widened * inv_rms * norm_gain).astype(jnp.bfloat16), inv_rms)

def gating(normed, router, route_ids):
    logits = jnp.dot(normed, router, preferred_element_type=jnp.float32)
    affinity = jax.nn.sigmoid(jnp.take_along_axis(logits, route_ids, axis=1))
    affinity_sum = lax.optimization_barrier(jnp.sum(affinity, axis=1, keepdims=True))
    return (affinity, affinity_sum, ROUTE_SCALE * affinity / affinity_sum)

def hidden_act(gate_pre, up_pre):
    return (jax.nn.silu(gate_pre) * up_pre).astype(jnp.bfloat16)

def slot_lists(route_ids):
    flat_ids = route_ids.reshape(-1)
    lists = []
    for expert in range(EXPERTS):
        picked = jnp.nonzero(flat_ids == expert, size=N_EXPERT * CAP, fill_value=flat_ids.shape[0])[0]
        lists.append(picked.astype(jnp.int32))
    return lists

def expert_inputs(normed_rows, w_gate, w_up):
    gate_pre = jnp.dot(to_float(normed_rows), to_float(w_gate), preferred_element_type=jnp.float32)
    up_pre = jnp.dot(to_float(normed_rows), to_float(w_up), preferred_element_type=jnp.float32)
    return (gate_pre, up_pre)

def layer_forward(inputs, norm_gain, router, w_gate, w_up, w_down, route_ids):
    token_count = inputs.shape[0]
    normed, inv_rms = normalize(inputs, norm_gain)
    affinity, affinity_sum, gates = gating(normed, router, route_ids)
    outputs = jnp.zeros((token_count * TOPK, D), jnp.bfloat16)
    for expert, picked in enumerate(slot_lists(route_ids)):
        first_unit = expert * EXP_HID
        token_index = jnp.minimum(picked // TOPK, token_count - 1).astype(jnp.int32)
        normed_rows = jnp.take(normed, token_index, axis=0)
        gate_pre, up_pre = expert_inputs(normed_rows, w_gate[:, first_unit:first_unit + EXP_HID], w_up[:, first_unit:first_unit + EXP_HID])
        hidden = hidden_act(gate_pre, up_pre)
        expert_out = jnp.dot(to_float(hidden), to_float(w_down[first_unit:first_unit + EXP_HID]), preferred_element_type=jnp.float32)
        outputs = outputs.at[picked].set(expert_out.astype(jnp.bfloat16), mode='drop')
    slot_values = to_float(outputs).reshape(token_count, TOPK, D)
    mixed_rows = to_float(inputs) + lax.optimization_barrier(jnp.sum(gates[:, :, None] * slot_values, axis=1))
    return mixed_rows.astype(jnp.bfloat16)

def layer_backward(inputs, cotangent, norm_gain, router, w_gate, w_up, w_down, route_ids):
    token_count = inputs.shape[0]
    normed, inv_rms = normalize(inputs, norm_gain)
    affinity, affinity_sum, gates = gating(normed, router, route_ids)
    partials = jnp.zeros((token_count * TOPK, D), jnp.bfloat16)
    sensitivity = jnp.zeros((token_count * TOPK,), jnp.float32)
    for expert, picked in enumerate(slot_lists(route_ids)):
        first_unit = expert * EXP_HID
        gate_cols = w_gate[:, first_unit:first_unit + EXP_HID]
        up_cols = w_up[:, first_unit:first_unit + EXP_HID]
        down_rows = w_down[first_unit:first_unit + EXP_HID]
        token_index = jnp.minimum(picked // TOPK, token_count - 1).astype(jnp.int32)
        normed_rows = jnp.take(normed, token_index, axis=0)
        cotangent_rows = jnp.take(cotangent, token_index, axis=0)
        gate_pre, up_pre = expert_inputs(normed_rows, gate_cols, up_cols)
        gate_sig = jax.nn.sigmoid(gate_pre)
        hidden = hidden_act(gate_pre, up_pre)
        hidden_grad = jnp.dot(to_float(cotangent_rows), to_float(down_rows).T, preferred_element_type=jnp.float32)
        slot_sens = lax.optimization_barrier(jnp.sum(to_float(hidden) * hidden_grad, axis=-1))
        gate_grad = (hidden_grad * up_pre * gate_sig * (1.0 + gate_pre * (1.0 - gate_sig))).astype(jnp.bfloat16)
        up_grad = (hidden_grad * jax.nn.silu(gate_pre)).astype(jnp.bfloat16)
        slot_grad = jnp.dot(to_float(gate_grad), to_float(gate_cols).T, preferred_element_type=jnp.float32)
        slot_grad = slot_grad + jnp.dot(to_float(up_grad), to_float(up_cols).T, preferred_element_type=jnp.float32)
        partials = partials.at[picked].set(slot_grad.astype(jnp.bfloat16), mode='drop')
        sensitivity = sensitivity.at[picked].set(slot_sens, mode='drop')
    part_slots = to_float(partials).reshape(token_count, TOPK, D)
    sens_slots = sensitivity.reshape(token_count, TOPK)
    weighted = lax.optimization_barrier(jnp.sum(affinity * sens_slots, axis=1, keepdims=True))
    logit_grad = ROUTE_SCALE / affinity_sum * (sens_slots - weighted / affinity_sum) * affinity * (1.0 - affinity)
    onehot = (route_ids[:, :, None] == jnp.arange(EXPERTS, dtype=jnp.int32)[None, None, :]).astype(jnp.float32)
    spread = lax.optimization_barrier(jnp.sum(logit_grad[:, :, None] * onehot, axis=1))
    normed_grad = lax.optimization_barrier(jnp.sum(gates[:, :, None] * part_slots, axis=1))
    normed_grad = normed_grad + jnp.einsum('re,de->rd', spread, to_float(router), precision=lax.Precision.HIGHEST)
    widened = to_float(inputs)
    scaled = norm_gain * normed_grad
    inner_sum = lax.optimization_barrier(jnp.sum(widened * scaled, axis=-1, keepdims=True)) / D
    result = to_float(cotangent) + inv_rms * scaled - widened * inv_rms ** 3 * inner_sum
    return result.astype(jnp.bfloat16)

def reference(act_in, grad_in, feed, loss_grad, saved, fwd_gain, fwd_router, fwd_gate, fwd_up, fwd_down, bwd_gain, bwd_router, bwd_gate, bwd_up, bwd_down, fwd_routes, bwd_routes):
    section_count = act_in.shape[0]
    forward_now = [act_in[section_index] for section_index in range(section_count)]
    backward_now = [grad_in[section_index] for section_index in range(section_count)]
    forward_ticks = []
    backward_ticks = []
    for step_index in range(TICKS):
        forward_done = [layer_forward(forward_now[section_index], fwd_gain[section_index], fwd_router[section_index], fwd_gate[section_index], fwd_up[section_index], fwd_down[section_index], fwd_routes[section_index, step_index]) for section_index in range(section_count)]
        backward_done = [layer_backward(saved[section_index, step_index], backward_now[section_index], bwd_gain[section_index], bwd_router[section_index], bwd_gate[section_index], bwd_up[section_index], bwd_down[section_index], bwd_routes[section_index, step_index]) for section_index in range(section_count)]
        forward_ticks.append(jnp.stack(forward_done))
        backward_ticks.append(jnp.stack(backward_done))
        if step_index + 1 < TICKS:
            forward_now = [feed[step_index]] + forward_done[:-1]
            backward_now = [loss_grad[step_index]] + backward_done[:-1]
    return (jnp.stack(forward_ticks, axis=1), jnp.stack(backward_ticks, axis=1))
```

```python
import functools
from typing import Any, NamedTuple

import jax
import jax.numpy as jnp
from jax import lax
from jax.experimental import pallas as pl
from jax.experimental.pallas import tpu as pltpu
from jax.sharding import PartitionSpec as P

NORM_EPS = 1e-06
ROUTE_SCALE = 2.5
MESH = pl.DeviceIdType.MESH
F32 = jnp.float32
BF16 = jnp.bfloat16
CHUNKS = 7
LINE = 4
AHEAD = 4


def dot(a, b):
    return jnp.dot(a, b, preferred_element_type=F32)


def dot_t(a, b):
    return lax.dot_general(a, b, (((1,), (1,)), ((), ())), preferred_element_type=F32)


def iota(shape, axis):
    return lax.broadcasted_iota(jnp.int32, shape, axis)


def split_dot(weights, values):
    high = weights.astype(BF16)
    low = (weights - high.astype(F32)).astype(BF16)
    return dot(high, values) + dot(low, values)


class Move:
    def __init__(self, src, dst, send, recv, device):
        self.copy = pltpu.make_async_remote_copy(
            src_ref=src, dst_ref=dst, send_sem=send, recv_sem=recv,
            device_id=device, device_id_type=MESH,
        )

    def start(self):
        self.copy.start()

    def recv(self):
        self.copy.wait_recv()

    def sent(self):
        self.copy.wait_send()


class Refs(NamedTuple):
    act: Any
    grad: Any
    feed: Any
    loss: Any
    saved: Any
    fgain: Any
    bgain: Any
    frouter: Any
    brouter: Any
    fgate: Any
    fup: Any
    fdown: Any
    bgate: Any
    bup: Any
    bdown: Any
    ids: Any
    out_f: Any
    out_b: Any
    xf0: Any
    xf1: Any
    xc: Any
    xs: Any
    tf: Any
    tn: Any
    pkf: Any
    pkn: Any
    pkc: Any
    rf: Any
    rn: Any
    rc: Any
    sf: Any
    sg: Any
    pf: Any
    pg: Any
    xif: Any
    xig: Any
    ysf: Any
    ysg: Any
    yrf: Any
    yrg: Any
    owf: Any
    owg: Any
    of: Any
    ob: Any
    wfg: Any
    wfu: Any
    wfd: Any
    wbg: Any
    wbu: Any
    wbd: Any
    ag: Any
    au: Any
    bg: Any
    bu: Any
    bh: Any
    hidden: Any
    gg: Any
    ug: Any
    seall: Any
    sep: Any
    ser: Any
    sex: Any
    sei: Any
    seys: Any
    seyr: Any
    seown: Any
    gaf: Any
    gan: Any
    rsn: Any
    idb: Any
    idall: Any
    idsend: Any
    idtb: Any
    ld_w: Any
    ld_x: Any
    ld_out: Any
    ysem_s: Any
    ysem_r: Any
    xsem_s: Any
    xsem_r: Any
    dsem_s: Any
    dsem_r: Any
    d2_s: Any
    d2_r: Any
    x2_s: Any
    x2_r: Any
    y2_s: Any
    y2_r: Any
    hop_s: Any
    hop_r: Any
    fy_s: Any
    sd_s: Any
    sd_r: Any
    sx_s: Any
    sx_r: Any
    sy_s: Any
    sy_r: Any
    id_s: Any
    id_r: Any


def kernel(dims, *refs):
    rows, width, cap, hid, sections = dims
    nc = CHUNKS
    cw = width // nc
    slots = 2 * cap
    line_rows = LINE * slots
    g = Refs(*refs)

    sec = lax.axis_index("section")
    me = lax.axis_index("expert")
    core = lax.rem(me, 2)
    x = lax.rem(me // 2, LINE)
    y = me // (2 * LINE)
    mate_index = lax.rem(me + 2 * LINE, 4 * LINE)
    sibling = (sec, me + 1 - 2 * core)
    mate = (sec, mate_index)

    def along(step):
        return (sec, (y * LINE + lax.rem(x + step, LINE)) * 2 + core)

    next_sec = lax.rem(sec + 1, sections)
    last_sec = lax.rem(sec + sections - 1, sections)
    first = sec == 0
    inner = sec != 0
    sender = sec != sections - 1
    own_rows = pl.ds(0, rows)
    mate_rows = pl.ds(rows, rows)
    own_part = pl.ds(0, line_rows)
    sibling_part = pl.ds(line_rows, line_rows)

    def cols(ch):
        return pl.ds(pl.multiple_of(ch * cw, cw), cw)

    def chunks(*bodies):
        @pl.loop(0, nc)
        def _(ch):
            for body in bodies:
                body(ch)

    loads = (
        (g.grad, g.xc.at[0, :, own_rows]), (g.saved.at[0], g.xs.at[0]), (g.act, g.xf0),
        (g.saved.at[1], g.xs.at[1]), (g.loss, g.xc.at[1, :, own_rows]), (g.feed, g.xf1.at[:, own_rows]),
    )
    cot_0, saved_0, act_0, saved_1, cot_1, act_1 = range(6)

    def load_start(k):
        src, dst = loads[k]
        chunks(lambda ch: pltpu.make_async_copy(src.at[:, cols(ch)], dst.at[ch], g.ld_x.at[k]).start())

    def load_wait(k):
        dst = loads[k][1]
        pltpu.make_async_copy(dst, dst, g.ld_x.at[k]).wait()

    weights = [
        pltpu.make_async_copy(src, dst, g.ld_w.at[k])
        for k, (src, dst) in enumerate((
            (g.bdown, g.wbd), (g.bgate, g.wbg), (g.bup, g.wbu),
            (g.fgate, g.wfg), (g.fup, g.wfu), (g.fdown, g.wfd),
        ))
    ]
    load_bdown, load_bgate, load_bup, load_fgate, load_fup, load_fdown = weights

    for k in (cot_0, saved_0, act_0, saved_1):
        load_start(k)

    @pl.when(first)
    def _():
        load_start(cot_1)
        load_start(act_1)

    for copy in weights:
        copy.start()

    barrier = pltpu.get_barrier_semaphore()
    partners = [sibling, mate] + [along(d) for d in (1, 2, 3)]
    partners += [(s, e) for s in (next_sec, last_sec) for e in (me, mate_index)]
    for device in partners:
        pl.semaphore_signal(barrier, inc=1, device_id=device, device_id_type=MESH)
    pl.semaphore_wait(barrier, len(partners))

    g.idsend[...] = pltpu.roll(g.ids[...], rows, 1)
    id_move = Move(g.idsend, g.idtb, g.id_s.at[0], g.id_r.at[0], mate)
    id_move.start()

    blocks = (g.tf, g.tn.at[0], g.tn.at[1], g.xc.at[0])
    packs = (g.pkf, g.pkn, g.pkn, g.pkc)
    arrivals = (g.rf, g.rn, g.rn, g.rc)

    shared_sem = (0, 1, 1, 2)
    far = pl.ds(slots, 3 * slots)

    def y_move(p, ch):
        t = blocks[p]
        return Move(t.at[ch, own_rows], t.at[ch, mate_rows], g.ysem_s.at[p], g.ysem_r.at[p, ch], mate)

    def x_move(p, ch, d):
        return Move(
            packs[p].at[ch, pl.ds((d - 1) * slots, slots)], arrivals[p].at[ch, pl.ds(d * slots, slots)],
            g.xsem_s.at[shared_sem[p]], g.xsem_r.at[shared_sem[p], ch], along(d),
        )

    def d_move(p, ch):
        r = arrivals[p]
        k = shared_sem[p]
        return Move(r.at[ch, own_part], r.at[ch, sibling_part], g.dsem_s.at[k], g.dsem_r.at[k, ch], sibling)

    def y_sent(p):
        block = blocks[p].at[:, own_rows]
        Move(block, block, g.ysem_s.at[p], g.ysem_r.at[p, 0], mate).sent()

    def packed_sent(p):
        k = shared_sem[p]
        Move(packs[p], packs[p], g.xsem_s.at[k], g.xsem_r.at[k, 0], mate).sent()

    def shared_sent(p):
        k = shared_sem[p]
        block = arrivals[p].at[:, own_part]
        Move(block, block, g.dsem_s.at[k], g.dsem_r.at[k, 0], sibling).sent()

    def y_recv(p):
        return lambda ch: y_move(p, ch).recv()

    def y_ahead(p, later):
        def body(ch):
            @pl.when(ch < nc - AHEAD)
            def _():
                y_move(p, ch + AHEAD).start()
            if later is not None:
                @pl.when(ch >= nc - AHEAD)
                def _():
                    y_move(later, ch + AHEAD - nc).start()
        return body

    def pack(p, block, placer):
        def body(ch):
            packed = dot(placer, block[ch]).astype(BF16)
            packs[p][ch] = packed[slots:]
            for d in (2, 1, 3):
                x_move(p, ch, d).start()
            arrivals[p][ch, 0:slots] = packed[0:slots]
        return body

    def share(p):
        def body(ch):
            k = shared_sem[p]
            block = arrivals[p].at[ch, far]
            Move(block, block, g.xsem_s.at[k], g.xsem_r.at[k, ch], mate).recv()
            d_move(p, ch).start()
        return body

    def norm_rows(load_chunk, gain, store_chunk):
        wide = [load_chunk(ch).astype(F32) for ch in range(nc)]
        total = sum(jnp.sum(v * v, axis=1, keepdims=True) for v in wide)
        inv_rms = lax.rsqrt(total / width + NORM_EPS)
        for ch, v in enumerate(wide):
            store_chunk(ch, (v * inv_rms * gain[:, ch * cw:(ch + 1) * cw]).astype(BF16))
        return inv_rms

    def packer(column):
        shape = (line_rows, 2 * rows)
        row, token = iota(shape, 0), iota(shape, 1)
        expert = y * LINE + lax.rem(x + row // slots, LINE)
        both = g.idall[...]
        named = (both[column:column + 1] == expert) | (both[column + 1:column + 2] == expert)
        up = (2 * rows, 2 * rows)
        tri = (iota(up, 0) < iota(up, 1)) & (iota(up, 0) // rows == iota(up, 1) // rows)
        place = dot(named.astype(F32).astype(BF16), tri.astype(F32).astype(BF16))
        within = lax.rem(row, slots)
        hit = named & (place == lax.rem(within, cap).astype(F32)) & (within // cap == token // rows)
        return hit.astype(F32).astype(BF16)

    def unpacker(column):
        shape = (2 * rows, line_rows)
        token, col = iota(shape, 0), iota(shape, 1)
        expert = y * LINE + lax.rem(x + col // slots, LINE)
        ids = g.idb[...]
        named0 = ids[:, column:column + 1] == expert
        named1 = ids[:, column + 1:column + 2] == expert
        low = (2 * rows, 2 * rows)
        tri = (iota(low, 1) < iota(low, 0)) & (iota(low, 0) // rows == iota(low, 1) // rows)
        place = dot(tri.astype(F32).astype(BF16), (named0 | named1).astype(F32).astype(BF16))
        within = lax.rem(col, slots)
        fits = (place == lax.rem(within, cap).astype(F32)) & (within // cap == token // rows)
        return (fits & named0).astype(F32), (fits & named1).astype(F32)

    def gating(t, router, column, store):
        logits = sum(dot_t(t[ch], router[:, ch * cw:(ch + 1) * cw]) for ch in range(nc))
        ids = g.idb[...]
        experts = iota(logits.shape, 1)
        aff = []
        for k in range(2):
            picked = jnp.where(ids[:, column + k:column + k + 1] == experts, logits, 0.0)
            aff.append(jax.nn.sigmoid(jnp.sum(picked, axis=1, keepdims=True)))
        total = aff[0] + aff[1]
        lane = iota((2 * rows, 128), 1)
        value = jnp.where(lane == 0, aff[0], jnp.where(lane == 1, aff[1], 0.0))
        value = jnp.where(lane == 2, ROUTE_SCALE * aff[0] / total, value)
        store[...] = jnp.where(lane == 3, ROUTE_SCALE * aff[1] / total, value)

    def gather_up(p, w_gate, w_up, acc_g, acc_u):
        def body(ch):
            d_move(p, ch).recv()
            acc_g[...] += dot(arrivals[p][ch], w_gate[cols(ch)])
            acc_u[...] += dot(arrivals[p][ch], w_up[cols(ch)])
        return body

    def gather_grad(ch):
        d_move(3, ch).recv()
        g.bh[...] += dot_t(g.rc[ch], g.wbd[:, cols(ch)])

    partial = (g.pf, g.pg)
    from_sibling = (g.sf, g.sg)
    returned = (g.xif, g.xig)
    own_sum = (g.owf, g.owg)
    to_mate = (g.ysf, g.ysg)
    from_mate = (g.yrf, g.yrg)
    results = (g.of, g.ob)
    inboxes = (g.xf1, g.xc.at[1])
    outs = (g.out_f, g.out_b)

    def d2_move(q, ch):
        return Move(partial[q].at[ch], from_sibling[q].at[ch], g.d2_s.at[q], g.d2_r.at[q, ch], sibling)

    def x2_move(q, ch, d):
        part = pl.ds(d * slots, slots)
        return Move(
            partial[q].at[ch, part], returned[q].at[ch, part],
            g.x2_s.at[q], g.x2_r.at[q, ch], along(LINE - d),
        )

    def y2_move(q, ch):
        return Move(to_mate[q].at[ch], from_mate[q].at[ch], g.y2_s.at[q], g.y2_r.at[q, ch], mate)

    def product(q, part, ch):
        if q == 0:
            return dot(g.hidden[part], g.wfd[:, cols(ch)])
        return dot_t(g.gg[part], g.wbg[cols(ch)]) + dot_t(g.ug[part], g.wbu[cols(ch)])

    def half_out(q):
        def body(ch):
            partial[q][ch] = product(q, sibling_part, ch).astype(BF16)
            d2_move(q, ch).start()
        return body

    def half_sent(q, payloads):
        Move(partial[q], partial[q], g.d2_s.at[q], g.d2_r.at[q, 0], sibling).sent()
        for p in payloads:
            shared_sent(p)

    def half_own(q):
        def body(ch):
            value = product(q, own_part, ch)
            d2_move(q, ch).recv()
            partial[q][ch] = (value + from_sibling[q][ch].astype(F32)).astype(BF16)
            for d in (2, 1, 3):
                x2_move(q, ch, d).start()
            returned[q][ch, 0:slots] = partial[q][ch, 0:slots]
        return body

    def combine(q, mix):
        def body(ch):
            block = returned[q].at[ch, far]
            Move(block, block, g.x2_s.at[q], g.x2_r.at[q, ch], mate).recv()
            mixed = split_dot(mix, returned[q][ch])
            own_sum[q][ch] = mixed[0:rows]
            to_mate[q][ch] = mixed[rows:].astype(BF16)
            y2_move(q, ch).start()
        return body

    def return_sent(q):
        block = partial[q].at[:, far]
        Move(block, block, g.x2_s.at[q], g.x2_r.at[q, 0], mate).sent()
        Move(to_mate[q], to_mate[q], g.y2_s.at[q], g.y2_r.at[q, 0], mate).sent()

    def hop_move(q, ch, other):
        target = (next_sec, mate_index if other else me)
        part = mate_rows if other else own_rows
        return Move(
            results[q].at[0, ch], inboxes[q].at[ch, part],
            g.hop_s.at[q, other], g.hop_r.at[q, other, ch], target,
        )

    def feed_move(q, ch):
        return Move(
            inboxes[q].at[ch, own_rows], inboxes[q].at[ch, mate_rows],
            g.fy_s.at[q], g.hop_r.at[q, 1, ch], mate,
        )

    def out_copy(q, tick, ch):
        return pltpu.make_async_copy(results[q].at[tick, ch], outs[q].at[tick, :, cols(ch)], g.ld_out.at[q])

    def deliver(q, tick, ch):
        if tick == 0:
            @pl.when(sender)
            def _():
                for other in (0, 1):
                    hop_move(q, ch, other).start()
        out_copy(q, tick, ch).start()

    def arrived(q):
        def body(ch):
            @pl.when(inner)
            def _():
                hop_move(q, ch, 0).recv()
            hop_move(q, ch, 1).recv()
        return body

    def sens_d():
        return Move(g.sep, g.ser, g.sd_s.at[0], g.sd_r.at[0], sibling)

    def sens_x(d):
        part = pl.ds(d * slots, slots)
        return Move(g.sex.at[part], g.sei.at[part], g.sx_s.at[0], g.sx_r.at[0], along(LINE - d))

    def sens_y():
        return Move(g.seys, g.seyr, g.sy_s.at[0], g.sy_r.at[0], mate)

    def mix_of(store, column):
        hit0, hit1 = unpacker(column)
        return hit0 * store[:, 2:3] + hit1 * store[:, 3:4], hit0, hit1

    def activate():
        @pl.loop(0, 2 * LINE)
        def _(n):
            part = pl.ds(pl.multiple_of(n * slots, 16), slots)
            pre = g.ag[part]
            g.hidden[part] = (pre * jax.nn.sigmoid(pre) * g.au[part]).astype(BF16)

    def forward_finish(tick):
        before = g.xf0 if tick == 0 else g.xf1

        def body(ch):
            y2_move(0, ch).recv()
            value = before[ch, 0:rows].astype(F32) + (g.owf[ch] + g.yrf[ch].astype(F32))
            g.of[tick, ch] = value.astype(BF16)
            deliver(0, tick, ch)
        chunks(body)

    def backward_act():
        @pl.loop(0, 2 * LINE)
        def _(n):
            part = pl.ds(pl.multiple_of(n * slots, 16), slots)
            pre, up, hgrad = g.bg[part], g.bu[part], g.bh[part]
            sig = jax.nn.sigmoid(pre)
            silu = pre * sig
            act = (silu * up).astype(BF16).astype(F32)
            sens = jnp.sum(act * hgrad, axis=1, keepdims=True)
            g.gg[part] = (hgrad * up * sig * (1.0 + pre * (1.0 - sig))).astype(BF16)
            g.ug[part] = (hgrad * silu).astype(BF16)
            g.seall[part] = jnp.broadcast_to(sens, (slots, 128))
        g.sep[...] = g.seall[line_rows:]
        sens_d().start()

    def sens_out():
        sens_d().sent()
        sens_d().recv()
        g.sex[...] = g.seall[0:line_rows] + g.ser[...]
        for d in (1, 2, 3):
            sens_x(d).start()
        g.sei[0:slots] = g.sex[0:slots]

    def sens_combine(hits):
        block = g.sei.at[far]
        Move(block, block, g.sx_s.at[0], g.sx_r.at[0], mate).recv()
        found = [
            jnp.dot(hit, g.sei[...], precision=lax.Precision.HIGHEST, preferred_element_type=F32)
            for hit in hits
        ]
        lane = iota((2 * rows, 128), 1)
        both = jnp.where(lane == 0, found[0], jnp.where(lane == 1, found[1], 0.0))
        g.seown[...] = both[0:rows]
        g.seys[...] = both[rows:]
        sens_y().start()

    def sens_sent():
        block = g.sex.at[far]
        Move(block, block, g.sx_s.at[0], g.sx_r.at[0], mate).sent()
        sens_y().sent()

    def backward_finish(tick):
        sens_y().recv()
        sens = g.seown[...] + g.seyr[...]
        store = g.gan.at[tick]
        aff = [store[0:rows, k:k + 1] for k in range(2)]
        total = aff[0] + aff[1]
        weighted = aff[0] * sens[:, 0:1] + aff[1] * sens[:, 1:2]
        column = 4 + 2 * tick
        ids = g.idb[0:rows]
        experts = iota((rows, 8), 1)
        spread = jnp.zeros((rows, 8), F32)
        for k in range(2):
            lgrad = ROUTE_SCALE / total * (sens[:, k:k + 1] - weighted / total) * aff[k] * (1.0 - aff[k])
            spread = spread + jnp.where(ids[:, column + k:column + k + 1] == experts, lgrad, 0.0)
        high = spread.astype(BF16)
        rest = spread - high.astype(F32)
        mid = rest.astype(BF16)
        low = (rest - mid.astype(F32)).astype(BF16)

        def gather(ch, inner_sum):
            router = g.brouter[:, cols(ch)]
            y2_move(1, ch).recv()
            ngrad = g.owg[ch] + g.yrg[ch].astype(F32)
            ngrad = ngrad + (dot(high, router) + dot(mid, router) + dot(low, router))
            scaled = g.bgain[:, cols(ch)] * ngrad
            g.owg[ch] = scaled
            return inner_sum + jnp.sum(g.xs[tick, ch].astype(F32) * scaled, axis=1, keepdims=True)

        inner_sum = lax.fori_loop(0, nc, gather, jnp.zeros((rows, 1), F32))
        inv_rms = g.rsn[tick][:, 0:1]
        factor = inv_rms * inv_rms * inv_rms * (inner_sum / width)

        def body(ch):
            value = g.xc[tick, ch, 0:rows].astype(F32) + inv_rms * g.owg[ch]
            value = value - g.xs[tick, ch].astype(F32) * factor
            g.ob[tick, ch] = value.astype(BF16)
            deliver(1, tick, ch)
        chunks(body)

    def clear(*sums):
        for ref in sums:
            ref[...] = jnp.zeros_like(ref)

    def norm_saved(tick):
        def store(ch, value):
            g.tn[tick, ch, 0:rows] = value
        inv_rms = norm_rows(lambda ch: g.xs[tick, ch], g.bgain, store)
        g.rsn[tick] = jnp.broadcast_to(inv_rms, (rows, 128))

    def norm_forward(block, base):
        def store(ch, value):
            g.tf[ch, base:base + rows] = value
        norm_rows(lambda ch: block[ch, base:base + rows], g.fgain, store)

    load_wait(cot_0)
    for ch in range(AHEAD):
        y_move(3, ch).start()
    id_move.recv()
    g.idall[...] = jnp.maximum(g.ids[...], g.idtb[...])
    g.idb[...] = g.idall[...].T
    placer_b = packer(4)
    load_wait(saved_0)
    norm_saved(0)
    chunks(y_recv(3), y_ahead(3, 1), pack(3, g.xc.at[0], placer_b))
    load_wait(act_0)
    norm_forward(g.xf0, 0)
    clear(g.bh, g.bg, g.bu, g.ag, g.au)
    chunks(y_recv(1), y_ahead(1, 0), pack(1, g.tn.at[0], placer_b), share(3))
    load_wait(saved_1)
    norm_saved(1)
    placer_f = packer(0)
    load_bdown.wait()
    chunks(y_recv(0), y_ahead(0, 2), share(1), pack(0, g.tf, placer_f), gather_grad)
    gating(g.tn.at[0], g.brouter, 4, g.gan.at[0])
    for ch in range(AHEAD, nc):
        y_move(2, ch).start()

    @pl.when(first)
    def _():
        for q, k in ((1, cot_1), (0, act_1)):
            load_wait(k)
            chunks(lambda ch, q=q: feed_move(q, ch).start())

    for tick in range(2):
        if tick == 0:
            load_bgate.wait()
            load_bup.wait()
            chunks(gather_up(1, g.wbg, g.wbu, g.bg, g.bu))
        backward_act()
        chunks(half_out(1))
        sens_out()
        half_sent(1, (1 + tick, 3))
        chunks(half_own(1), share(0))
        if tick == 0:
            gating(g.tf, g.frouter, 0, g.gaf)
            load_fgate.wait()
            load_fup.wait()
        chunks(gather_up(0, g.wfg, g.wfu, g.ag, g.au))
        activate()
        if tick == 0:
            load_fdown.wait()
        chunks(half_out(0))
        mix, hit0, hit1 = mix_of(g.gan.at[tick], 4 + 2 * tick)
        sens_combine((hit0, hit1))
        half_sent(0, (0,))
        chunks(combine(1, mix), half_own(0))
        backward_finish(tick)
        mix, _, _ = mix_of(g.gaf, 2 * tick)
        if tick == 1:
            chunks(combine(0, mix))
            forward_finish(1)
            break
        placer_b = packer(6)
        packed_sent(1)
        clear(g.bh, g.bg, g.bu, g.ag, g.au)
        chunks(combine(0, mix), y_recv(2), pack(2, g.tn.at[1], placer_b))
        forward_finish(0)
        packed_sent(3)
        packed_sent(0)
        return_sent(0)
        return_sent(1)
        y_sent(0)
        sens_sent()
        chunks(arrived(1), pack(3, g.xc.at[1], placer_b), share(2))
        gating(g.tn.at[1], g.brouter, 6, g.gan.at[1])
        chunks(gather_up(2, g.wbg, g.wbu, g.bg, g.bu))
        chunks(arrived(0))
        norm_forward(g.xf1, 0)
        norm_forward(g.xf1, rows)
        placer_f = packer(2)
        chunks(pack(0, g.tf, placer_f), share(3))
        gating(g.tf, g.frouter, 2, g.gaf)
        chunks(gather_grad)

    for p in (0, 2, 3):
        packed_sent(p)
    for p in (1, 2, 3):
        y_sent(p)
    return_sent(0)
    return_sent(1)
    sens_sent()
    id_move.sent()

    @pl.when(sender)
    def _():
        for q in range(2):
            for other in range(2):
                block = results[q].at[0]
                Move(block, block, g.hop_s.at[q, other], g.hop_r.at[q, other, 0], mate).sent()

    @pl.when(first)
    def _():
        for q in range(2):
            block = inboxes[q].at[:, own_rows]
            Move(block, block, g.fy_s.at[q], g.hop_r.at[q, 1, 0], mate).sent()

    for q in range(2):
        pltpu.make_async_copy(results[q], results[q], g.ld_out.at[q]).wait()


def copy_kernel(a, b, out_a, out_b, held, sems):
    moves = [
        (src.at[tick], held.at[2 * k + tick], dst.at[tick], 2 * k + tick)
        for k, (src, dst) in enumerate(((a, out_a), (b, out_b))) for tick in range(2)
    ]
    into = [pltpu.make_async_copy(src, slot, sems.at[0, n]) for src, slot, dst, n in moves]
    back = [pltpu.make_async_copy(slot, dst, sems.at[1, n]) for src, slot, dst, n in moves]
    for copy in into:
        copy.start()
    for first_leg, second_leg in zip(into, back):
        first_leg.wait()
        second_leg.start()
    for copy in back:
        copy.wait()


def per_device(
    act_in, grad_in, feed, loss_grad, saved,
    fwd_gain, fwd_router, fwd_gate, fwd_up, fwd_down,
    bwd_gain, bwd_router, bwd_gate, bwd_up, bwd_down,
    fwd_routes, bwd_routes,
):
    rows, width = act_in.shape[1:]
    hid = fwd_gate.shape[2]
    experts = fwd_router.shape[2]
    cap = rows * fwd_routes.shape[3] // experts + rows // 8
    sections = lax.axis_size("section")
    nc = CHUNKS
    cw = width // nc
    slots = 2 * cap
    line = LINE * slots

    ids = jnp.concatenate([fwd_routes[0], bwd_routes[0]]).transpose(0, 2, 1).reshape(8, rows)
    ids = jnp.pad(ids, ((0, 0), (0, rows)), constant_values=-1)

    any_spec = pl.BlockSpec(memory_space=pl.ANY)
    vmem_spec = pl.BlockSpec(memory_space=pltpu.VMEM)

    def b(*shape):
        return pltpu.VMEM(shape, BF16)

    def f(*shape):
        return pltpu.VMEM(shape, F32)

    def i(*shape):
        return pltpu.VMEM(shape, jnp.int32)

    def dma(*shape):
        return pltpu.SemaphoreType.DMA(shape)

    scratch = [
        b(nc, rows, cw), b(nc, 2 * rows, cw), b(2, nc, 2 * rows, cw), b(2, nc, rows, cw),
        b(nc, 2 * rows, cw), b(2, nc, 2 * rows, cw),
        b(nc, 3 * slots, cw), b(nc, 3 * slots, cw), b(nc, 3 * slots, cw),
        b(nc, 2 * line, cw), b(nc, 2 * line, cw), b(nc, 2 * line, cw),
        b(nc, line, cw), b(nc, line, cw), b(nc, line, cw), b(nc, line, cw),
        b(nc, line, cw), b(nc, line, cw),
        b(nc, rows, cw), b(nc, rows, cw), b(nc, rows, cw), b(nc, rows, cw),
        f(nc, rows, cw), f(nc, rows, cw),
        b(2, nc, rows, cw), b(2, nc, rows, cw),
        b(width, hid), b(width, hid), b(hid, width),
        b(width, hid), b(width, hid), b(hid, width),
        f(2 * line, hid), f(2 * line, hid), f(2 * line, hid), f(2 * line, hid), f(2 * line, hid),
        b(2 * line, hid), b(2 * line, hid), b(2 * line, hid),
        f(2 * line, 128),
        f(line, 128), f(line, 128), f(line, 128), f(line, 128),
        f(rows, 128), f(rows, 128), f(rows, 128),
        f(2 * rows, 128), f(2, 2 * rows, 128), f(2, rows, 128),
        i(2 * rows, 8), i(8, 2 * rows), i(8, 2 * rows), i(8, 2 * rows),
        dma(6), dma(6), dma(2),
        dma(4), dma(4, nc), dma(3), dma(3, nc), dma(3), dma(3, nc),
        dma(2), dma(2, nc), dma(2), dma(2, nc), dma(2), dma(2, nc),
        dma(2, 2), dma(2, 2, nc), dma(2),
        dma(1), dma(1), dma(1), dma(1), dma(1), dma(1), dma(1), dma(1),
    ]
    out_shape = jax.ShapeDtypeStruct((2, rows, width), BF16)
    call = pl.pallas_call(
        functools.partial(kernel, (rows, width, cap, hid, sections)),
        out_shape=(out_shape, out_shape),
        in_specs=[any_spec] * 5 + [vmem_spec] * 4 + [any_spec] * 6 + [vmem_spec],
        out_specs=(any_spec, any_spec),
        scratch_shapes=scratch,
        compiler_params=pltpu.CompilerParams(
            collective_id=0, has_side_effects=True, vmem_limit_bytes=63 * 2**20
        ),
    )
    out_f, out_b = call(
        act_in[0], grad_in[0], feed[0], loss_grad[0], saved[0],
        fwd_gain, bwd_gain, fwd_router[0].T, bwd_router[0].T,
        fwd_gate[0], fwd_up[0], fwd_down[0], bwd_gate[0], bwd_up[0], bwd_down[0],
        ids,
    )
    out_f, out_b = pl.pallas_call(
        copy_kernel,
        out_shape=(out_shape, out_shape),
        in_specs=[any_spec] * 2,
        out_specs=(any_spec, any_spec),
        scratch_shapes=[b(4, rows, width), dma(2, 4)],
    )(out_f, out_b)
    return out_f[None], out_b[None]


def solution(mesh):
    in_specs = (
        P("section", "expert", None),
        P("section", "expert", None),
        P(None, "expert", None),
        P(None, "expert", None),
        P("section", None, "expert", None),
        P("section", None),
        P("section", None, None),
        P("section", None, "expert"),
        P("section", None, "expert"),
        P("section", "expert", None),
        P("section", None),
        P("section", None, None),
        P("section", None, "expert"),
        P("section", None, "expert"),
        P("section", "expert", None),
        P("section", None, "expert", None),
        P("section", None, "expert", None),
    )
    out_specs = (P("section", None, "expert", None), P("section", None, "expert", None))
    return jax.shard_map(
        per_device, mesh=mesh, in_specs=in_specs, out_specs=out_specs, check_vma=False
    )
```

```python
import functools
from typing import Any, NamedTuple

import jax
import jax.numpy as jnp
from jax import lax
from jax.experimental import pallas as pl
from jax.experimental.pallas import tpu as pltpu
from jax.sharding import PartitionSpec as P

NORM_EPS = 1e-06
ROUTE_SCALE = 2.5
MESH = pl.DeviceIdType.MESH
F32 = jnp.float32
BF16 = jnp.bfloat16
CHUNKS = 7
LINE = 4
AHEAD = 5
HEAD = CHUNKS - AHEAD


def dot(a, b):
    return jnp.dot(a, b, preferred_element_type=F32)


def dot_t(a, b):
    return lax.dot_general(a, b, (((1,), (1,)), ((), ())), preferred_element_type=F32)


def iota(shape, axis):
    return lax.broadcasted_iota(jnp.int32, shape, axis)


def split_dot(weights, values):
    high = weights.astype(BF16)
    low = (weights - high.astype(F32)).astype(BF16)
    return dot(high, values) + dot(low, values)


class Move:
    def __init__(self, src, dst, send, recv, device):
        self.copy = pltpu.make_async_remote_copy(
            src_ref=src, dst_ref=dst, send_sem=send, recv_sem=recv,
            device_id=device, device_id_type=MESH,
        )

    def start(self):
        self.copy.start()

    def recv(self):
        self.copy.wait_recv()

    def sent(self):
        self.copy.wait_send()


class Refs(NamedTuple):
    act: Any
    grad: Any
    feed: Any
    loss: Any
    saved: Any
    fgain: Any
    bgain: Any
    frouter: Any
    brouter: Any
    fgate: Any
    fup: Any
    fdown: Any
    bgate: Any
    bup: Any
    bdown: Any
    ids: Any
    out_f: Any
    out_b: Any
    xf0: Any
    xf1: Any
    xc: Any
    xs: Any
    tf: Any
    tn: Any
    pkf: Any
    pkn: Any
    pkc: Any
    rf: Any
    rn: Any
    rc: Any
    sf: Any
    sg: Any
    pf: Any
    pg: Any
    xif: Any
    xig: Any
    ysf: Any
    ysg: Any
    yrf: Any
    yrg: Any
    owf: Any
    owg: Any
    of: Any
    ob: Any
    wfg: Any
    wfu: Any
    wfd: Any
    wbg: Any
    wbu: Any
    wbd: Any
    ag: Any
    au: Any
    bg: Any
    bu: Any
    bh: Any
    hidden: Any
    gg: Any
    ug: Any
    seall: Any
    sep: Any
    ser: Any
    sex: Any
    sei: Any
    seys: Any
    seyr: Any
    seown: Any
    gaf: Any
    gan: Any
    rsn: Any
    zs: Any
    zr: Any
    idb: Any
    idall: Any
    idsend: Any
    idtb: Any
    ld_w: Any
    ld_x: Any
    ld_out: Any
    ysem_s: Any
    ysem_r: Any
    xsem_s: Any
    xsem_r: Any
    dsem_s: Any
    dsem_r: Any
    d2_s: Any
    d2_r: Any
    x2_s: Any
    x2_r: Any
    y2_s: Any
    y2_r: Any
    hop_s: Any
    hop_r: Any
    fy_s: Any
    sd_s: Any
    sd_r: Any
    sx_s: Any
    sx_r: Any
    sy_s: Any
    sy_r: Any
    id_s: Any
    id_r: Any
    ga_s: Any
    ga_r: Any
    zsem_s: Any
    zsem_r: Any


def kernel(dims, *refs):
    rows, width, cap, hid, sections = dims
    nc = CHUNKS
    cw = width // nc
    slots = 2 * cap
    line_rows = LINE * slots
    g = Refs(*refs)

    sec = lax.axis_index("section")
    me = lax.axis_index("expert")
    core = lax.rem(me, 2)
    x = lax.rem(me // 2, LINE)
    y = me // (2 * LINE)
    mate_index = lax.rem(me + 2 * LINE, 4 * LINE)
    sibling = (sec, me + 1 - 2 * core)
    mate = (sec, mate_index)

    def along(step):
        return (sec, (y * LINE + lax.rem(x + step, LINE)) * 2 + core)

    next_sec = lax.rem(sec + 1, sections)
    last_sec = lax.rem(sec + sections - 1, sections)
    first = sec == 0
    inner = sec != 0
    even = lax.rem(sec, 2) == 0
    odd = jnp.logical_not(even)
    sender = sec != sections - 1
    own_rows = pl.ds(0, rows)
    mate_rows = pl.ds(rows, rows)
    own_part = pl.ds(0, line_rows)
    sibling_part = pl.ds(line_rows, line_rows)

    def cols(ch):
        return pl.ds(pl.multiple_of(ch * cw, cw), cw)

    def chunks(*bodies, start=0, stop=nc):
        @pl.loop(start, stop)
        def _(ch):
            for body in bodies:
                body(ch)

    loads = (
        (g.grad, g.xc.at[0, :, own_rows]), (g.saved.at[0], g.xs.at[0]), (g.act, g.xf0),
        (g.saved.at[1], g.xs.at[1]), (g.loss, g.xc.at[1, :, own_rows]), (g.feed, g.xf1.at[:, own_rows]),
    )
    cot_0, saved_0, act_0, saved_1, cot_1, act_1 = range(6)

    def load_start(k):
        src, dst = loads[k]
        chunks(lambda ch: pltpu.make_async_copy(src.at[:, cols(ch)], dst.at[ch], g.ld_x.at[k]).start())

    def load_wait(k):
        dst = loads[k][1]
        pltpu.make_async_copy(dst, dst, g.ld_x.at[k]).wait()

    weights = [
        pltpu.make_async_copy(src, dst, g.ld_w.at[k])
        for k, (src, dst) in enumerate((
            (g.bgate, g.wbg), (g.bup, g.wbu), (g.bdown, g.wbd),
            (g.fgate, g.wfg), (g.fup, g.wfu), (g.fdown, g.wfd),
        ))
    ]
    load_bgate, load_bup, load_bdown, load_fgate, load_fup, load_fdown = weights

    for k in (saved_0, cot_0, act_0, saved_1):
        load_start(k)

    @pl.when(first)
    def _():
        load_start(cot_1)
        load_start(act_1)

    barrier = pltpu.get_barrier_semaphore()
    partners = [sibling, mate] + [along(d) for d in (1, 2, 3)]
    partners += [(s, e) for s in (next_sec, last_sec) for e in (me, mate_index)]
    for device in partners:
        pl.semaphore_signal(barrier, inc=1, device_id=device, device_id_type=MESH)

    g.idsend[...] = pltpu.roll(g.ids[...], rows, 1)
    id_move = Move(g.idsend, g.idtb, g.id_s.at[0], g.id_r.at[0], mate)

    blocks = (g.tf, g.tn.at[0], g.tn.at[1], g.xc.at[0])
    packs = (g.pkf, g.pkn, g.pkn, g.pkc)
    arrivals = (g.rf, g.rn, g.rn, g.rc)

    shared_sem = (0, 1, 1, 2)
    far = pl.ds(slots, 3 * slots)

    def y_move(p, ch):
        t = blocks[p]
        return Move(t.at[ch, own_rows], t.at[ch, mate_rows], g.ysem_s.at[p], g.ysem_r.at[p, ch], mate)

    def z_move(ch):
        return Move(g.zs.at[ch], g.zr.at[ch], g.zsem_s.at[0], g.zsem_r.at[ch], mate)

    def x_move(p, ch, d):
        return Move(
            packs[p].at[ch, pl.ds((d - 1) * slots, slots)], arrivals[p].at[ch, pl.ds(d * slots, slots)],
            g.xsem_s.at[shared_sem[p]], g.xsem_r.at[shared_sem[p], ch], along(d),
        )

    def d_move(p, ch):
        r = arrivals[p]
        k = shared_sem[p]
        return Move(r.at[ch, own_part], r.at[ch, sibling_part], g.dsem_s.at[k], g.dsem_r.at[k, ch], sibling)

    def y_sent(p):
        block = blocks[p].at[pl.ds(HEAD, nc - HEAD) if p == 1 else pl.ds(0, nc), own_rows]
        Move(block, block, g.ysem_s.at[p], g.ysem_r.at[p, 0], mate).sent()

    def z_sent():
        Move(g.zs, g.zs, g.zsem_s.at[0], g.zsem_r.at[0], mate).sent()

    def packed_sent(p):
        k = shared_sem[p]
        Move(packs[p], packs[p], g.xsem_s.at[k], g.xsem_r.at[k, 0], mate).sent()

    def shared_sent(p):
        k = shared_sem[p]
        block = arrivals[p].at[:, own_part]
        Move(block, block, g.dsem_s.at[k], g.dsem_r.at[k, 0], sibling).sent()

    def y_recv(p):
        return lambda ch: y_move(p, ch).recv()

    def y_ahead(p, later):
        def body(ch):
            @pl.when(ch < nc - AHEAD)
            def _():
                y_move(p, ch + AHEAD).start()
            if later is not None:
                @pl.when(ch >= nc - AHEAD)
                def _():
                    y_move(later, ch + AHEAD - nc).start()
        return body

    def pack(p, block, placer):
        def body(ch):
            packed = dot(placer, block[ch]).astype(BF16)
            packs[p][ch] = packed[slots:]
            for d in (2, 1, 3):
                x_move(p, ch, d).start()
            arrivals[p][ch, 0:slots] = packed[0:slots]
        return body

    def x_recv(p, ch):
        block = arrivals[p].at[ch, far]
        Move(block, block, g.xsem_s.at[shared_sem[p]], g.xsem_r.at[shared_sem[p], ch], mate).recv()

    def share(p):
        def body(ch):
            x_recv(p, ch)
            d_move(p, ch).start()
        return body

    def swap_out(p):
        shape = (line_rows // 2, line_rows)
        row, col = iota(shape, 0), iota(shape, 1)
        other = (col == row // cap * slots + cap + lax.rem(row, cap)).astype(F32).astype(BF16)

        def body(ch):
            x_recv(p, ch)
            g.zs[ch] = dot(other, g.rn[ch, 0:line_rows]).astype(BF16)
            z_move(ch).start()
        return body

    def swap_in(p):
        shape = (line_rows, line_rows // 2)
        row, col = iota(shape, 0), iota(shape, 1)
        place = (row == col // cap * slots + cap + lax.rem(col, cap)).astype(F32).astype(BF16)

        def body(ch):
            z_move(ch).recv()
            swapped = dot(place, g.zr[ch])
            mine = lax.rem(iota(swapped.shape, 0), slots) < cap
            g.rn[ch, 0:line_rows] = jnp.where(mine, g.rn[ch, 0:line_rows].astype(F32), swapped).astype(BF16)
            d_move(p, ch).start()
        return body

    def norm_rows(load_chunk, gain, store_chunk):
        wide = [load_chunk(ch).astype(F32) for ch in range(nc)]
        total = sum(jnp.sum(v * v, axis=1, keepdims=True) for v in wide)
        inv_rms = lax.rsqrt(total / width + NORM_EPS)
        for ch, v in enumerate(wide):
            store_chunk(ch, (v * inv_rms * gain[:, ch * cw:(ch + 1) * cw]).astype(BF16))
        return inv_rms

    def packer(column):
        shape = (line_rows, 2 * rows)
        row, token = iota(shape, 0), iota(shape, 1)
        expert = y * LINE + lax.rem(x + row // slots, LINE)
        both = g.idall[...]
        named = (both[column:column + 1] == expert) | (both[column + 1:column + 2] == expert)
        up = (2 * rows, 2 * rows)
        tri = (iota(up, 0) < iota(up, 1)) & (iota(up, 0) // rows == iota(up, 1) // rows)
        place = dot(named.astype(F32).astype(BF16), tri.astype(F32).astype(BF16))
        within = lax.rem(row, slots)
        hit = named & (place == lax.rem(within, cap).astype(F32)) & (within // cap == token // rows)
        return hit.astype(F32).astype(BF16)

    def own_packer(column):
        shape = (line_rows, 2 * rows)
        row, token = iota(shape, 0), iota(shape, 1)
        within = lax.rem(row, slots)
        expert = lax.rem(y + within // cap, 2) * LINE + lax.rem(x + row // slots, LINE)
        ids = g.ids[...]
        named = (ids[column:column + 1] == expert) | (ids[column + 1:column + 2] == expert)
        up = (2 * rows, 2 * rows)
        tri = iota(up, 0) < iota(up, 1)
        place = dot(named.astype(F32).astype(BF16), tri.astype(F32).astype(BF16))
        hit = named & (place == lax.rem(within, cap).astype(F32))
        return hit.astype(F32).astype(BF16)[:, 0:rows]

    def unpacker(column):
        shape = (2 * rows, line_rows)
        token, col = iota(shape, 0), iota(shape, 1)
        expert = y * LINE + lax.rem(x + col // slots, LINE)
        ids = g.idb[...]
        named0 = ids[:, column:column + 1] == expert
        named1 = ids[:, column + 1:column + 2] == expert
        low = (2 * rows, 2 * rows)
        tri = (iota(low, 1) < iota(low, 0)) & (iota(low, 0) // rows == iota(low, 1) // rows)
        place = dot(tri.astype(F32).astype(BF16), (named0 | named1).astype(F32).astype(BF16))
        within = lax.rem(col, slots)
        fits = (place == lax.rem(within, cap).astype(F32)) & (within // cap == token // rows)
        return (fits & named0).astype(F32), (fits & named1).astype(F32)

    def gating(t, router, column, store):
        logits = sum(dot_t(t[ch], router[:, ch * cw:(ch + 1) * cw]) for ch in range(nc))
        count = logits.shape[0]
        ids = g.idb[0:count]
        experts = iota(logits.shape, 1)
        aff = []
        for k in range(2):
            picked = jnp.where(ids[:, column + k:column + k + 1] == experts, logits, 0.0)
            aff.append(jax.nn.sigmoid(jnp.sum(picked, axis=1, keepdims=True)))
        total = aff[0] + aff[1]
        lane = iota((count, 128), 1)
        value = jnp.where(lane == 0, aff[0], jnp.where(lane == 1, aff[1], 0.0))
        value = jnp.where(lane == 2, ROUTE_SCALE * aff[0] / total, value)
        store[...] = jnp.where(lane == 3, ROUTE_SCALE * aff[1] / total, value)

    def gather_up(p, w_gate, w_up, acc_g, acc_u):
        def body(ch):
            d_move(p, ch).recv()
            acc_g[...] += dot(arrivals[p][ch], w_gate[cols(ch)])
            acc_u[...] += dot(arrivals[p][ch], w_up[cols(ch)])
        return body

    def gather_grad(ch):
        d_move(3, ch).recv()
        g.bh[...] += dot_t(g.rc[ch], g.wbd[:, cols(ch)])

    partial = (g.pf, g.pg)
    from_sibling = (g.sf, g.sg)
    returned = (g.xif, g.xig)
    own_sum = (g.owf, g.owg)
    to_mate = (g.ysf, g.ysg)
    from_mate = (g.yrf, g.yrg)
    results = (g.of, g.ob)
    inboxes = (g.xf1, g.xc.at[1])
    outs = (g.out_f, g.out_b)

    def d2_move(q, ch):
        return Move(partial[q].at[ch], from_sibling[q].at[ch], g.d2_s.at[q], g.d2_r.at[q, ch], sibling)

    def x2_move(q, ch, d):
        part = pl.ds(d * slots, slots)
        return Move(
            partial[q].at[ch, part], returned[q].at[ch, part],
            g.x2_s.at[q], g.x2_r.at[q, ch], along(LINE - d),
        )

    def y2_move(q, ch):
        return Move(to_mate[q].at[ch], from_mate[q].at[ch], g.y2_s.at[q], g.y2_r.at[q, ch], mate)

    def product(q, part, ch):
        if q == 0:
            return dot(g.hidden[part], g.wfd[:, cols(ch)])
        return dot_t(g.gg[part], g.wbg[cols(ch)]) + dot_t(g.ug[part], g.wbu[cols(ch)])

    def half_out(q):
        def body(ch):
            partial[q][ch] = product(q, sibling_part, ch).astype(BF16)
            d2_move(q, ch).start()
        return body

    def half_sent(q, payloads):
        Move(partial[q], partial[q], g.d2_s.at[q], g.d2_r.at[q, 0], sibling).sent()
        for p in payloads:
            shared_sent(p)

    def half_own(q):
        def body(ch):
            value = product(q, own_part, ch)
            d2_move(q, ch).recv()
            partial[q][ch] = (value + from_sibling[q][ch].astype(F32)).astype(BF16)
            for d in (2, 1, 3):
                x2_move(q, ch, d).start()
            returned[q][ch, 0:slots] = partial[q][ch, 0:slots]
        return body

    def combine(q, mix):
        def body(ch):
            block = returned[q].at[ch, far]
            Move(block, block, g.x2_s.at[q], g.x2_r.at[q, ch], mate).recv()
            mixed = split_dot(mix, returned[q][ch])
            own_sum[q][ch] = mixed[0:rows]
            to_mate[q][ch] = mixed[rows:].astype(BF16)
            y2_move(q, ch).start()
        return body

    def return_sent(q):
        block = partial[q].at[:, far]
        Move(block, block, g.x2_s.at[q], g.x2_r.at[q, 0], mate).sent()
        Move(to_mate[q], to_mate[q], g.y2_s.at[q], g.y2_r.at[q, 0], mate).sent()

    def hop_move(q, ch, other):
        target = (next_sec, mate_index if other else me)
        part = mate_rows if other else own_rows
        return Move(
            results[q].at[0, ch], inboxes[q].at[ch, part],
            g.hop_s.at[q, other], g.hop_r.at[q, other, ch], target,
        )

    def feed_move(q, ch):
        return Move(
            inboxes[q].at[ch, own_rows], inboxes[q].at[ch, mate_rows],
            g.fy_s.at[q], g.hop_r.at[q, 1, ch], mate,
        )

    def out_copy(q, tick, ch):
        return pltpu.make_async_copy(results[q].at[tick, ch], outs[q].at[tick, :, cols(ch)], g.ld_out.at[q])

    def deliver(q, tick, ch):
        if tick == 0:
            @pl.when(sender)
            def _():
                hop_move(q, ch, 0).start()

            @pl.when(sender & even if q == 0 else sender)
            def _():
                hop_move(q, ch, 1).start()
        out_copy(q, tick, ch).start()

    def arrived(q):
        def body(ch):
            @pl.when(inner)
            def _():
                hop_move(q, ch, 0).recv()
            if q == 1:
                hop_move(q, ch, 1).recv()
            else:
                pl.when(odd)(hop_move(q, ch, 1).recv)
        return body

    def sens_d():
        return Move(g.sep, g.ser, g.sd_s.at[0], g.sd_r.at[0], sibling)

    def sens_x(d):
        part = pl.ds(d * slots, slots)
        return Move(g.sex.at[part], g.sei.at[part], g.sx_s.at[0], g.sx_r.at[0], along(LINE - d))

    def sens_y():
        return Move(g.seys, g.seyr, g.sy_s.at[0], g.sy_r.at[0], mate)

    def mix_of(store, column):
        hit0, hit1 = unpacker(column)
        return hit0 * store[:, 2:3] + hit1 * store[:, 3:4], hit0, hit1

    def activate():
        @pl.loop(0, 2 * LINE)
        def _(n):
            part = pl.ds(pl.multiple_of(n * slots, 16), slots)
            pre = g.ag[part]
            g.hidden[part] = (pre * jax.nn.sigmoid(pre) * g.au[part]).astype(BF16)

    def forward_finish(tick):
        before = g.xf0 if tick == 0 else g.xf1

        def body(ch):
            y2_move(0, ch).recv()
            value = before[ch, 0:rows].astype(F32) + (g.owf[ch] + g.yrf[ch].astype(F32))
            g.of[tick, ch] = value.astype(BF16)
            deliver(0, tick, ch)
        chunks(body)

    def backward_act():
        @pl.loop(0, 2 * LINE)
        def _(n):
            part = pl.ds(pl.multiple_of(n * slots, 16), slots)
            pre, up, hgrad = g.bg[part], g.bu[part], g.bh[part]
            sig = jax.nn.sigmoid(pre)
            silu = pre * sig
            act = (silu * up).astype(BF16).astype(F32)
            sens = jnp.sum(act * hgrad, axis=1, keepdims=True)
            g.gg[part] = (hgrad * up * sig * (1.0 + pre * (1.0 - sig))).astype(BF16)
            g.ug[part] = (hgrad * silu).astype(BF16)
            g.seall[part] = jnp.broadcast_to(sens, (slots, 128))
        g.sep[...] = g.seall[line_rows:]
        sens_d().start()

    def sens_out():
        sens_d().sent()
        sens_d().recv()
        g.sex[...] = g.seall[0:line_rows] + g.ser[...]
        for d in (1, 2, 3):
            sens_x(d).start()
        g.sei[0:slots] = g.sex[0:slots]

    def sens_combine(hits):
        block = g.sei.at[far]
        Move(block, block, g.sx_s.at[0], g.sx_r.at[0], mate).recv()
        found = [
            jnp.dot(hit, g.sei[...], precision=lax.Precision.HIGHEST, preferred_element_type=F32)
            for hit in hits
        ]
        lane = iota((2 * rows, 128), 1)
        both = jnp.where(lane == 0, found[0], jnp.where(lane == 1, found[1], 0.0))
        g.seown[...] = both[0:rows]
        g.seys[...] = both[rows:]
        sens_y().start()

    def sens_sent():
        block = g.sex.at[far]
        Move(block, block, g.sx_s.at[0], g.sx_r.at[0], mate).sent()
        sens_y().sent()

    def backward_finish(tick):
        sens_y().recv()
        sens = g.seown[...] + g.seyr[...]
        store = g.gan.at[tick]
        aff = [store[0:rows, k:k + 1] for k in range(2)]
        total = aff[0] + aff[1]
        weighted = aff[0] * sens[:, 0:1] + aff[1] * sens[:, 1:2]
        column = 4 + 2 * tick
        ids = g.idb[0:rows]
        experts = iota((rows, 8), 1)
        spread = jnp.zeros((rows, 8), F32)
        for k in range(2):
            lgrad = ROUTE_SCALE / total * (sens[:, k:k + 1] - weighted / total) * aff[k] * (1.0 - aff[k])
            spread = spread + jnp.where(ids[:, column + k:column + k + 1] == experts, lgrad, 0.0)
        high = spread.astype(BF16)
        rest = spread - high.astype(F32)
        mid = rest.astype(BF16)
        low = (rest - mid.astype(F32)).astype(BF16)

        def gather(ch, inner_sum):
            router = g.brouter[:, cols(ch)]
            y2_move(1, ch).recv()
            ngrad = g.owg[ch] + g.yrg[ch].astype(F32)
            ngrad = ngrad + (dot(high, router) + dot(mid, router) + dot(low, router))
            scaled = g.bgain[:, cols(ch)] * ngrad
            g.owg[ch] = scaled
            return inner_sum + jnp.sum(g.xs[tick, ch].astype(F32) * scaled, axis=1, keepdims=True)

        inner_sum = lax.fori_loop(0, nc, gather, jnp.zeros((rows, 1), F32))
        inv_rms = g.rsn[tick][:, 0:1]
        factor = inv_rms * inv_rms * inv_rms * (inner_sum / width)

        def body(ch):
            value = g.xc[tick, ch, 0:rows].astype(F32) + inv_rms * g.owg[ch]
            value = value - g.xs[tick, ch].astype(F32) * factor
            g.ob[tick, ch] = value.astype(BF16)
            deliver(1, tick, ch)
        chunks(body)

    def clear(*sums):
        for ref in sums:
            ref[...] = jnp.zeros_like(ref)

    def norm_saved(tick):
        def store(ch, value):
            g.tn[tick, ch, 0:rows] = value
        inv_rms = norm_rows(lambda ch: g.xs[tick, ch], g.bgain, store)
        g.rsn[tick] = jnp.broadcast_to(inv_rms, (rows, 128))

    def norm_forward(block, base):
        def store(ch, value):
            g.tf[ch, base:base + rows] = value
        norm_rows(lambda ch: block[ch, base:base + rows], g.fgain, store)

    def gate_move(tick):
        store = g.gan.at[tick]
        return Move(store.at[own_rows], store.at[mate_rows], g.ga_s.at[tick], g.ga_r.at[tick], mate)

    def gate_saved(tick):
        gating(g.tn.at[tick, :, own_rows], g.brouter, 4 + 2 * tick, g.gan.at[tick, own_rows])
        gate_move(tick).start()

    load_wait(saved_0)
    norm_saved(0)
    placer_n = own_packer(4)
    load_wait(cot_0)
    pl.semaphore_wait(barrier, len(partners))
    id_move.start()
    chunks(lambda ch: y_move(1, ch).start(), start=HEAD)
    chunks(pack(1, g.tn.at[0, :, own_rows], placer_n), stop=HEAD)
    for copy in weights:
        copy.start()
    id_move.recv()
    g.idall[...] = jnp.maximum(g.ids[...], g.idtb[...])
    g.idb[...] = g.idall[...].T
    placer_b = packer(4)
    chunks(
        y_recv(1), lambda ch: y_move(3, ch - HEAD).start(), pack(1, g.tn.at[0], placer_b), start=HEAD,
    )
    load_wait(act_0)
    norm_forward(g.xf0, 0)
    chunks(y_recv(3), y_ahead(3, 0), pack(3, g.xc.at[0], placer_b), swap_out(1), stop=HEAD)
    chunks(y_recv(3), y_ahead(3, 0), pack(3, g.xc.at[0], placer_b), share(1), start=HEAD)
    clear(g.bh, g.bg, g.bu, g.ag, g.au)
    placer_f = packer(0)
    load_wait(saved_1)
    norm_saved(1)
    chunks(swap_in(1), stop=HEAD)
    load_bgate.wait()
    load_bup.wait()
    chunks(
        y_recv(0), y_ahead(0, 2), share(3), pack(0, g.tf, placer_f),
        gather_up(1, g.wbg, g.wbu, g.bg, g.bu),
    )
    for ch in range(AHEAD, nc):
        y_move(2, ch).start()
    load_bdown.wait()
    chunks(gather_grad)

    @pl.when(first)
    def _():
        load_wait(act_1)
        load_wait(cot_1)
        chunks(lambda ch: feed_move(1, ch).start())

    for tick in range(2):
        backward_act()
        chunks(half_out(1))
        sens_out()
        half_sent(1, (1 + tick, 3))
        chunks(half_own(1), share(0))
        if tick == 0:
            gate_saved(0)
            gate_saved(1)
            gating(g.tf, g.frouter, 0, g.gaf)
            load_fgate.wait()
            load_fup.wait()
        chunks(gather_up(0, g.wfg, g.wfu, g.ag, g.au))
        activate()
        if tick == 0:
            load_fdown.wait()
        chunks(half_out(0))
        gate_move(tick).recv()
        mix, hit0, hit1 = mix_of(g.gan.at[tick], 4 + 2 * tick)
        sens_combine((hit0, hit1))
        half_sent(0, (0,))
        chunks(combine(1, mix), half_own(0))
        backward_finish(tick)
        mix, _, _ = mix_of(g.gaf, 2 * tick)
        if tick == 1:
            chunks(combine(0, mix))
            forward_finish(1)
            break
        placer_b = packer(6)
        packed_sent(1)
        clear(g.bh, g.bg, g.bu, g.ag, g.au)
        chunks(combine(0, mix), y_recv(2), pack(2, g.tn.at[1], placer_b))
        forward_finish(0)
        packed_sent(3)
        packed_sent(0)
        return_sent(0)
        return_sent(1)
        y_sent(0)
        sens_sent()
        chunks(arrived(1), pack(3, g.xc.at[1], placer_b), share(2))
        chunks(arrived(0))
        norm_forward(g.xf1, 0)

        @pl.when(even)
        def _():
            chunks(lambda ch: y_move(0, ch).start())

        @pl.when(odd)
        def _():
            norm_forward(g.xf1, rows)

        placer_f = packer(2)
        chunks(lambda ch: pl.when(even)(y_move(0, ch).recv), pack(0, g.tf, placer_f), share(3), gather_up(2, g.wbg, g.wbu, g.bg, g.bu))
        gating(g.tf, g.frouter, 2, g.gaf)
        chunks(gather_grad)

    for p in (0, 2, 3):
        packed_sent(p)
    for p in (1, 2, 3):
        y_sent(p)
    z_sent()
    for tick in range(2):
        gate_move(tick).sent()
    return_sent(0)
    return_sent(1)
    sens_sent()
    id_move.sent()

    def hop_sent(q, other):
        block = results[q].at[0]
        Move(block, block, g.hop_s.at[q, other], g.hop_r.at[q, other, 0], mate).sent()

    @pl.when(sender)
    def _():
        hop_sent(0, 0)
        hop_sent(1, 0)
        hop_sent(1, 1)

    @pl.when(sender & even)
    def _():
        hop_sent(0, 1)

    @pl.when(even)
    def _():
        y_sent(0)

    @pl.when(first)
    def _():
        block = inboxes[1].at[:, own_rows]
        Move(block, block, g.fy_s.at[1], g.hop_r.at[1, 1, 0], mate).sent()

    for q in range(2):
        pltpu.make_async_copy(results[q], results[q], g.ld_out.at[q]).wait()


def copy_kernel(a, b, out_a, out_b, held, sems):
    moves = [
        (src.at[tick], held.at[2 * k + tick], dst.at[tick], 2 * k + tick)
        for k, (src, dst) in enumerate(((a, out_a), (b, out_b))) for tick in range(2)
    ]
    into = [pltpu.make_async_copy(src, slot, sems.at[0, n]) for src, slot, dst, n in moves]
    back = [pltpu.make_async_copy(slot, dst, sems.at[1, n]) for src, slot, dst, n in moves]
    for copy in into:
        copy.start()
    for first_leg, second_leg in zip(into, back):
        first_leg.wait()
        second_leg.start()
    for copy in back:
        copy.wait()


def per_device(
    act_in, grad_in, feed, loss_grad, saved,
    fwd_gain, fwd_router, fwd_gate, fwd_up, fwd_down,
    bwd_gain, bwd_router, bwd_gate, bwd_up, bwd_down,
    fwd_routes, bwd_routes,
):
    rows, width = act_in.shape[1:]
    hid = fwd_gate.shape[2]
    experts = fwd_router.shape[2]
    cap = rows * fwd_routes.shape[3] // experts + rows // 8
    sections = lax.axis_size("section")
    nc = CHUNKS
    cw = width // nc
    slots = 2 * cap
    line = LINE * slots

    ids = jnp.concatenate([fwd_routes[0], bwd_routes[0]]).transpose(0, 2, 1).reshape(8, rows)
    ids = jnp.pad(ids, ((0, 0), (0, rows)), constant_values=-1)

    any_spec = pl.BlockSpec(memory_space=pl.ANY)
    vmem_spec = pl.BlockSpec(memory_space=pltpu.VMEM)

    def b(*shape):
        return pltpu.VMEM(shape, BF16)

    def f(*shape):
        return pltpu.VMEM(shape, F32)

    def i(*shape):
        return pltpu.VMEM(shape, jnp.int32)

    def dma(*shape):
        return pltpu.SemaphoreType.DMA(shape)

    scratch = [
        b(nc, rows, cw), b(nc, 2 * rows, cw), b(2, nc, 2 * rows, cw), b(2, nc, rows, cw),
        b(nc, 2 * rows, cw), b(2, nc, 2 * rows, cw),
        b(nc, 3 * slots, cw), b(nc, 3 * slots, cw), b(nc, 3 * slots, cw),
        b(nc, 2 * line, cw), b(nc, 2 * line, cw), b(nc, 2 * line, cw),
        b(nc, line, cw), b(nc, line, cw), b(nc, line, cw), b(nc, line, cw),
        b(nc, line, cw), b(nc, line, cw),
        b(nc, rows, cw), b(nc, rows, cw), b(nc, rows, cw), b(nc, rows, cw),
        f(nc, rows, cw), f(nc, rows, cw),
        b(2, nc, rows, cw), b(2, nc, rows, cw),
        b(width, hid), b(width, hid), b(hid, width),
        b(width, hid), b(width, hid), b(hid, width),
        f(2 * line, hid), f(2 * line, hid), f(2 * line, hid), f(2 * line, hid), f(2 * line, hid),
        b(2 * line, hid), b(2 * line, hid), b(2 * line, hid),
        f(2 * line, 128),
        f(line, 128), f(line, 128), f(line, 128), f(line, 128),
        f(rows, 128), f(rows, 128), f(rows, 128),
        f(2 * rows, 128), f(2, 2 * rows, 128), f(2, rows, 128),
        b(HEAD, line // 2, cw), b(HEAD, line // 2, cw),
        i(2 * rows, 8), i(8, 2 * rows), i(8, 2 * rows), i(8, 2 * rows),
        dma(6), dma(6), dma(2),
        dma(4), dma(4, nc), dma(3), dma(3, nc), dma(3), dma(3, nc),
        dma(2), dma(2, nc), dma(2), dma(2, nc), dma(2), dma(2, nc),
        dma(2, 2), dma(2, 2, nc), dma(2),
        dma(1), dma(1), dma(1), dma(1), dma(1), dma(1), dma(1), dma(1), dma(2), dma(2), dma(1), dma(HEAD),
    ]
    out_shape = jax.ShapeDtypeStruct((2, rows, width), BF16)
    call = pl.pallas_call(
        functools.partial(kernel, (rows, width, cap, hid, sections)),
        out_shape=(out_shape, out_shape),
        in_specs=[any_spec] * 5 + [vmem_spec] * 4 + [any_spec] * 6 + [vmem_spec],
        out_specs=(any_spec, any_spec),
        scratch_shapes=scratch,
        compiler_params=pltpu.CompilerParams(
            collective_id=0, has_side_effects=True, vmem_limit_bytes=63 * 2**20
        ),
    )
    out_f, out_b = call(
        act_in[0], grad_in[0], feed[0], loss_grad[0], saved[0],
        fwd_gain, bwd_gain, fwd_router[0].T, bwd_router[0].T,
        fwd_gate[0], fwd_up[0], fwd_down[0], bwd_gate[0], bwd_up[0], bwd_down[0],
        ids,
    )
    out_f, out_b = pl.pallas_call(
        copy_kernel,
        out_shape=(out_shape, out_shape),
        in_specs=[any_spec] * 2,
        out_specs=(any_spec, any_spec),
        scratch_shapes=[b(4, rows, width), dma(2, 4)],
    )(out_f, out_b)
    return out_f[None], out_b[None]


def solution(mesh):
    in_specs = (
        P("section", "expert", None),
        P("section", "expert", None),
        P(None, "expert", None),
        P(None, "expert", None),
        P("section", None, "expert", None),
        P("section", None),
        P("section", None, None),
        P("section", None, "expert"),
        P("section", None, "expert"),
        P("section", "expert", None),
        P("section", None),
        P("section", None, None),
        P("section", None, "expert"),
        P("section", None, "expert"),
        P("section", "expert", None),
        P("section", None, "expert", None),
        P("section", None, "expert", None),
    )
    out_specs = (P("section", None, "expert", None), P("section", None, "expert", None))
    return jax.shard_map(
        per_device, mesh=mesh, in_specs=in_specs, out_specs=out_specs, check_vma=False
    )
```

```python
import functools
from typing import Any, NamedTuple

import jax
import jax.numpy as jnp
from jax import lax
from jax.experimental import pallas as pl
from jax.experimental.pallas import tpu as pltpu
from jax.sharding import PartitionSpec as P

NORM_EPS = 1e-06
ROUTE_SCALE = 2.5
MESH = pl.DeviceIdType.MESH
F32 = jnp.float32
BF16 = jnp.bfloat16
CHUNKS = 7
LINE = 4
AHEAD = 5
HEAD = CHUNKS - AHEAD


def dot(a, b):
    return jnp.dot(a, b, preferred_element_type=F32)


def dot_t(a, b):
    return lax.dot_general(a, b, (((1,), (1,)), ((), ())), preferred_element_type=F32)


def iota(shape, axis):
    return lax.broadcasted_iota(jnp.int32, shape, axis)


def split_dot(weights, values):
    high = weights.astype(BF16)
    low = (weights - high.astype(F32)).astype(BF16)
    return dot(high, values) + dot(low, values)


class Move:
    def __init__(self, src, dst, send, recv, device):
        self.copy = pltpu.make_async_remote_copy(
            src_ref=src, dst_ref=dst, send_sem=send, recv_sem=recv,
            device_id=device, device_id_type=MESH,
        )

    def start(self):
        self.copy.start()

    def recv(self):
        self.copy.wait_recv()

    def sent(self):
        self.copy.wait_send()


class Refs(NamedTuple):
    act: Any
    grad: Any
    feed: Any
    loss: Any
    saved: Any
    fgain_in: Any
    bgain_in: Any
    frouter_in: Any
    brouter_in: Any
    fgate: Any
    fup: Any
    fdown: Any
    bgate: Any
    bup: Any
    bdown: Any
    ids_in: Any
    out_f: Any
    out_b: Any
    xf0: Any
    xf1: Any
    xc: Any
    xs: Any
    tf: Any
    tn: Any
    pkf: Any
    pkn: Any
    pkc: Any
    rf: Any
    rn: Any
    rc: Any
    sf: Any
    sg: Any
    pf: Any
    pg: Any
    xif: Any
    xig: Any
    ysf: Any
    ysg: Any
    yrf: Any
    yrg: Any
    owf: Any
    owg: Any
    of: Any
    ob: Any
    wfg: Any
    wfu: Any
    wfd: Any
    wbg: Any
    wbu: Any
    wbd: Any
    ag: Any
    au: Any
    bg: Any
    bu: Any
    bh: Any
    hidden: Any
    gg: Any
    ug: Any
    seall: Any
    sep: Any
    ser: Any
    sex: Any
    sei: Any
    seys: Any
    seyr: Any
    seown: Any
    gaf: Any
    gan: Any
    rsn: Any
    fgain: Any
    bgain: Any
    frouter: Any
    brouter: Any
    ids: Any
    zs: Any
    zr: Any
    idb: Any
    idall: Any
    idsend: Any
    idtb: Any
    ld_w: Any
    ld_x: Any
    ld_out: Any
    ysem_s: Any
    ysem_r: Any
    xsem_s: Any
    xsem_r: Any
    dsem_s: Any
    dsem_r: Any
    d2_s: Any
    d2_r: Any
    x2_s: Any
    x2_r: Any
    y2_s: Any
    y2_r: Any
    hop_s: Any
    hop_r: Any
    fy_s: Any
    sd_s: Any
    sd_r: Any
    sx_s: Any
    sx_r: Any
    sy_s: Any
    sy_r: Any
    id_s: Any
    id_r: Any
    ga_s: Any
    ga_r: Any
    zsem_s: Any
    zsem_r: Any
    ld_s: Any


def kernel(dims, *refs):
    rows, width, cap, hid, sections = dims
    nc = CHUNKS
    cw = width // nc
    slots = 2 * cap
    line_rows = LINE * slots
    g = Refs(*refs)

    sec = lax.axis_index("section")
    me = lax.axis_index("expert")
    core = lax.rem(me, 2)
    x = lax.rem(me // 2, LINE)
    y = me // (2 * LINE)
    mate_index = lax.rem(me + 2 * LINE, 4 * LINE)
    sibling = (sec, me + 1 - 2 * core)
    mate = (sec, mate_index)

    def along(step):
        return (sec, (y * LINE + lax.rem(x + step, LINE)) * 2 + core)

    next_sec = lax.rem(sec + 1, sections)
    last_sec = lax.rem(sec + sections - 1, sections)
    first = sec == 0
    inner = sec != 0
    even = lax.rem(sec, 2) == 0
    odd = jnp.logical_not(even)
    sender = sec != sections - 1
    own_rows = pl.ds(0, rows)
    mate_rows = pl.ds(rows, rows)
    own_part = pl.ds(0, line_rows)
    sibling_part = pl.ds(line_rows, line_rows)

    def cols(ch):
        return pl.ds(pl.multiple_of(ch * cw, cw), cw)

    def chunks(*bodies, start=0, stop=nc):
        @pl.loop(start, stop)
        def _(ch):
            for body in bodies:
                body(ch)

    loads = (
        (g.grad, g.xc.at[0, :, own_rows]), (g.saved.at[0], g.xs.at[0]), (g.act, g.xf0),
        (g.saved.at[1], g.xs.at[1]), (g.loss, g.xc.at[1, :, own_rows]), (g.feed, g.xf1.at[:, own_rows]),
    )
    cot_0, saved_0, act_0, saved_1, cot_1, act_1 = range(6)

    def load_start(k):
        src, dst = loads[k]
        chunks(lambda ch: pltpu.make_async_copy(src.at[:, cols(ch)], dst.at[ch], g.ld_x.at[k]).start())

    def load_wait(k):
        dst = loads[k][1]
        pltpu.make_async_copy(dst, dst, g.ld_x.at[k]).wait()

    weights = [
        pltpu.make_async_copy(src, dst, g.ld_w.at[k])
        for k, (src, dst) in enumerate((
            (g.bgate, g.wbg), (g.bup, g.wbu), (g.bdown, g.wbd),
            (g.fgate, g.wfg), (g.fup, g.wfu), (g.fdown, g.wfd),
        ))
    ]
    load_bgate, load_bup, load_bdown, load_fgate, load_fup, load_fdown = weights

    small = [
        pltpu.make_async_copy(src, dst, g.ld_s.at[k])
        for k, (src, dst) in enumerate((
            (g.ids_in, g.ids), (g.bgain_in, g.bgain), (g.fgain_in, g.fgain),
            (g.brouter_in, g.brouter), (g.frouter_in, g.frouter),
        ))
    ]
    for copy in small[:2]:
        copy.start()
    for k in (saved_0, cot_0, act_0, saved_1):
        load_start(k)
    for copy in small[2:]:
        copy.start()

    @pl.when(first)
    def _():
        load_start(cot_1)
        load_start(act_1)

    barrier = pltpu.get_barrier_semaphore()
    partners = [sibling, mate] + [along(d) for d in (1, 2, 3)]
    partners += [(s, e) for s in (next_sec, last_sec) for e in (me, mate_index)]
    for device in partners:
        pl.semaphore_signal(barrier, inc=1, device_id=device, device_id_type=MESH)

    for copy in small[:2]:
        copy.wait()
    g.idsend[...] = pltpu.roll(g.ids[...], rows, 1)
    id_move = Move(g.idsend, g.idtb, g.id_s.at[0], g.id_r.at[0], mate)

    blocks = (g.tf, g.tn.at[0], g.tn.at[1], g.xc.at[0])
    packs = (g.pkf, g.pkn, g.pkn, g.pkc)
    arrivals = (g.rf, g.rn, g.rn, g.rc)

    shared_sem = (0, 1, 1, 2)
    far = pl.ds(slots, 3 * slots)

    def y_move(p, ch):
        t = blocks[p]
        return Move(t.at[ch, own_rows], t.at[ch, mate_rows], g.ysem_s.at[p], g.ysem_r.at[p, ch], mate)

    def z_move(ch):
        return Move(g.zs.at[ch], g.zr.at[ch], g.zsem_s.at[0], g.zsem_r.at[ch], mate)

    def x_move(p, ch, d):
        return Move(
            packs[p].at[ch, pl.ds((d - 1) * slots, slots)], arrivals[p].at[ch, pl.ds(d * slots, slots)],
            g.xsem_s.at[shared_sem[p]], g.xsem_r.at[shared_sem[p], ch], along(d),
        )

    def d_move(p, ch):
        r = arrivals[p]
        k = shared_sem[p]
        return Move(r.at[ch, own_part], r.at[ch, sibling_part], g.dsem_s.at[k], g.dsem_r.at[k, ch], sibling)

    def y_sent(p):
        block = blocks[p].at[pl.ds(HEAD, nc - HEAD) if p == 1 else pl.ds(0, nc), own_rows]
        Move(block, block, g.ysem_s.at[p], g.ysem_r.at[p, 0], mate).sent()

    def z_sent():
        Move(g.zs, g.zs, g.zsem_s.at[0], g.zsem_r.at[0], mate).sent()

    def packed_sent(p):
        k = shared_sem[p]
        Move(packs[p], packs[p], g.xsem_s.at[k], g.xsem_r.at[k, 0], mate).sent()

    def shared_sent(p):
        k = shared_sem[p]
        block = arrivals[p].at[:, own_part]
        Move(block, block, g.dsem_s.at[k], g.dsem_r.at[k, 0], sibling).sent()

    def y_recv(p):
        return lambda ch: y_move(p, ch).recv()

    def y_ahead(p, later):
        def body(ch):
            @pl.when(ch < nc - AHEAD)
            def _():
                y_move(p, ch + AHEAD).start()
            if later is not None:
                @pl.when(ch >= nc - AHEAD)
                def _():
                    y_move(later, ch + AHEAD - nc).start()
        return body

    def pack(p, block, placer):
        def body(ch):
            packed = dot(placer, block[ch]).astype(BF16)
            packs[p][ch] = packed[slots:]
            for d in (2, 1, 3):
                x_move(p, ch, d).start()
            arrivals[p][ch, 0:slots] = packed[0:slots]
        return body

    def x_recv(p, ch):
        block = arrivals[p].at[ch, far]
        Move(block, block, g.xsem_s.at[shared_sem[p]], g.xsem_r.at[shared_sem[p], ch], mate).recv()

    def share(p):
        def body(ch):
            x_recv(p, ch)
            d_move(p, ch).start()
        return body

    def swap_out(p):
        shape = (line_rows // 2, line_rows)
        row, col = iota(shape, 0), iota(shape, 1)
        other = (col == row // cap * slots + cap + lax.rem(row, cap)).astype(F32).astype(BF16)

        def body(ch):
            x_recv(p, ch)
            g.zs[ch] = dot(other, g.rn[ch, 0:line_rows]).astype(BF16)
            z_move(ch).start()
        return body

    def swap_in(p):
        shape = (line_rows, line_rows // 2)
        row, col = iota(shape, 0), iota(shape, 1)
        place = (row == col // cap * slots + cap + lax.rem(col, cap)).astype(F32).astype(BF16)

        def body(ch):
            z_move(ch).recv()
            swapped = dot(place, g.zr[ch])
            mine = lax.rem(iota(swapped.shape, 0), slots) < cap
            g.rn[ch, 0:line_rows] = jnp.where(mine, g.rn[ch, 0:line_rows].astype(F32), swapped).astype(BF16)
            d_move(p, ch).start()
        return body

    def norm_rows(load_chunk, gain, store_chunk):
        wide = [load_chunk(ch).astype(F32) for ch in range(nc)]
        total = sum(jnp.sum(v * v, axis=1, keepdims=True) for v in wide)
        inv_rms = lax.rsqrt(total / width + NORM_EPS)
        for ch, v in enumerate(wide):
            store_chunk(ch, (v * inv_rms * gain[:, ch * cw:(ch + 1) * cw]).astype(BF16))
        return inv_rms

    def packer(column):
        shape = (line_rows, 2 * rows)
        row, token = iota(shape, 0), iota(shape, 1)
        expert = y * LINE + lax.rem(x + row // slots, LINE)
        both = g.idall[...]
        named = (both[column:column + 1] == expert) | (both[column + 1:column + 2] == expert)
        up = (2 * rows, 2 * rows)
        tri = (iota(up, 0) < iota(up, 1)) & (iota(up, 0) // rows == iota(up, 1) // rows)
        place = dot(named.astype(F32).astype(BF16), tri.astype(F32).astype(BF16))
        within = lax.rem(row, slots)
        hit = named & (place == lax.rem(within, cap).astype(F32)) & (within // cap == token // rows)
        return hit.astype(F32).astype(BF16)

    def own_packer(column):
        shape = (line_rows, 2 * rows)
        row, token = iota(shape, 0), iota(shape, 1)
        within = lax.rem(row, slots)
        expert = lax.rem(y + within // cap, 2) * LINE + lax.rem(x + row // slots, LINE)
        ids = g.ids[...]
        named = (ids[column:column + 1] == expert) | (ids[column + 1:column + 2] == expert)
        up = (2 * rows, 2 * rows)
        tri = iota(up, 0) < iota(up, 1)
        place = dot(named.astype(F32).astype(BF16), tri.astype(F32).astype(BF16))
        hit = named & (place == lax.rem(within, cap).astype(F32))
        return hit.astype(F32).astype(BF16)[:, 0:rows]

    def unpacker(column):
        shape = (2 * rows, line_rows)
        token, col = iota(shape, 0), iota(shape, 1)
        expert = y * LINE + lax.rem(x + col // slots, LINE)
        ids = g.idb[...]
        named0 = ids[:, column:column + 1] == expert
        named1 = ids[:, column + 1:column + 2] == expert
        low = (2 * rows, 2 * rows)
        tri = (iota(low, 1) < iota(low, 0)) & (iota(low, 0) // rows == iota(low, 1) // rows)
        place = dot(tri.astype(F32).astype(BF16), (named0 | named1).astype(F32).astype(BF16))
        within = lax.rem(col, slots)
        fits = (place == lax.rem(within, cap).astype(F32)) & (within // cap == token // rows)
        return (fits & named0).astype(F32), (fits & named1).astype(F32)

    def gating(t, router, column, store):
        logits = sum(dot_t(t[ch], router[:, ch * cw:(ch + 1) * cw]) for ch in range(nc))
        count = logits.shape[0]
        ids = g.idb[0:count]
        experts = iota(logits.shape, 1)
        aff = []
        for k in range(2):
            picked = jnp.where(ids[:, column + k:column + k + 1] == experts, logits, 0.0)
            aff.append(jax.nn.sigmoid(jnp.sum(picked, axis=1, keepdims=True)))
        total = aff[0] + aff[1]
        lane = iota((count, 128), 1)
        value = jnp.where(lane == 0, aff[0], jnp.where(lane == 1, aff[1], 0.0))
        value = jnp.where(lane == 2, ROUTE_SCALE * aff[0] / total, value)
        store[...] = jnp.where(lane == 3, ROUTE_SCALE * aff[1] / total, value)

    def gather_up(p, w_gate, w_up, acc_g, acc_u):
        def body(ch):
            d_move(p, ch).recv()
            acc_g[...] += dot(arrivals[p][ch], w_gate[cols(ch)])
            acc_u[...] += dot(arrivals[p][ch], w_up[cols(ch)])
        return body

    def gather_grad(ch):
        d_move(3, ch).recv()
        g.bh[...] += dot_t(g.rc[ch], g.wbd[:, cols(ch)])

    partial = (g.pf, g.pg)
    from_sibling = (g.sf, g.sg)
    returned = (g.xif, g.xig)
    own_sum = (g.owf, g.owg)
    to_mate = (g.ysf, g.ysg)
    from_mate = (g.yrf, g.yrg)
    results = (g.of, g.ob)
    inboxes = (g.xf1, g.xc.at[1])
    outs = (g.out_f, g.out_b)

    def d2_move(q, ch):
        return Move(partial[q].at[ch], from_sibling[q].at[ch], g.d2_s.at[q], g.d2_r.at[q, ch], sibling)

    def x2_move(q, ch, d):
        part = pl.ds(d * slots, slots)
        return Move(
            partial[q].at[ch, part], returned[q].at[ch, part],
            g.x2_s.at[q], g.x2_r.at[q, ch], along(LINE - d),
        )

    def y2_move(q, ch):
        return Move(to_mate[q].at[ch], from_mate[q].at[ch], g.y2_s.at[q], g.y2_r.at[q, ch], mate)

    def product(q, part, ch):
        if q == 0:
            return dot(g.hidden[part], g.wfd[:, cols(ch)])
        return dot_t(g.gg[part], g.wbg[cols(ch)]) + dot_t(g.ug[part], g.wbu[cols(ch)])

    def half_out(q):
        def body(ch):
            partial[q][ch] = product(q, sibling_part, ch).astype(BF16)
            d2_move(q, ch).start()
        return body

    def half_sent(q, payloads):
        Move(partial[q], partial[q], g.d2_s.at[q], g.d2_r.at[q, 0], sibling).sent()
        for p in payloads:
            shared_sent(p)

    def half_own(q):
        def body(ch):
            value = product(q, own_part, ch)
            d2_move(q, ch).recv()
            partial[q][ch] = (value + from_sibling[q][ch].astype(F32)).astype(BF16)
            for d in (2, 1, 3):
                x2_move(q, ch, d).start()
            returned[q][ch, 0:slots] = partial[q][ch, 0:slots]
        return body

    def combine(q, mix):
        def body(ch):
            block = returned[q].at[ch, far]
            Move(block, block, g.x2_s.at[q], g.x2_r.at[q, ch], mate).recv()
            mixed = split_dot(mix, returned[q][ch])
            own_sum[q][ch] = mixed[0:rows]
            to_mate[q][ch] = mixed[rows:].astype(BF16)
            y2_move(q, ch).start()
        return body

    def return_sent(q):
        block = partial[q].at[:, far]
        Move(block, block, g.x2_s.at[q], g.x2_r.at[q, 0], mate).sent()
        Move(to_mate[q], to_mate[q], g.y2_s.at[q], g.y2_r.at[q, 0], mate).sent()

    def hop_move(q, ch, other):
        target = (next_sec, mate_index if other else me)
        part = mate_rows if other else own_rows
        return Move(
            results[q].at[0, ch], inboxes[q].at[ch, part],
            g.hop_s.at[q, other], g.hop_r.at[q, other, ch], target,
        )

    def feed_move(q, ch):
        return Move(
            inboxes[q].at[ch, own_rows], inboxes[q].at[ch, mate_rows],
            g.fy_s.at[q], g.hop_r.at[q, 1, ch], mate,
        )

    def out_copy(q, tick, ch):
        return pltpu.make_async_copy(results[q].at[tick, ch], outs[q].at[tick, :, cols(ch)], g.ld_out.at[q])

    def deliver(q, tick, ch):
        if tick == 0:
            @pl.when(sender)
            def _():
                hop_move(q, ch, 0).start()

            @pl.when(sender & even if q == 0 else sender)
            def _():
                hop_move(q, ch, 1).start()
        out_copy(q, tick, ch).start()

    def arrived(q):
        def body(ch):
            @pl.when(inner)
            def _():
                hop_move(q, ch, 0).recv()
            if q == 1:
                hop_move(q, ch, 1).recv()
            else:
                pl.when(odd)(hop_move(q, ch, 1).recv)
        return body

    def sens_d():
        return Move(g.sep, g.ser, g.sd_s.at[0], g.sd_r.at[0], sibling)

    def sens_x(d):
        part = pl.ds(d * slots, slots)
        return Move(g.sex.at[part], g.sei.at[part], g.sx_s.at[0], g.sx_r.at[0], along(LINE - d))

    def sens_y():
        return Move(g.seys, g.seyr, g.sy_s.at[0], g.sy_r.at[0], mate)

    def mix_of(store, column):
        hit0, hit1 = unpacker(column)
        return hit0 * store[:, 2:3] + hit1 * store[:, 3:4], hit0, hit1

    def activate():
        @pl.loop(0, 2 * LINE)
        def _(n):
            part = pl.ds(pl.multiple_of(n * slots, 16), slots)
            pre = g.ag[part]
            g.hidden[part] = (pre * jax.nn.sigmoid(pre) * g.au[part]).astype(BF16)

    def forward_finish(tick):
        before = g.xf0 if tick == 0 else g.xf1

        def body(ch):
            y2_move(0, ch).recv()
            value = before[ch, 0:rows].astype(F32) + (g.owf[ch] + g.yrf[ch].astype(F32))
            g.of[tick, ch] = value.astype(BF16)
            deliver(0, tick, ch)
        chunks(body)

    def backward_act():
        @pl.loop(0, 2 * LINE)
        def _(n):
            part = pl.ds(pl.multiple_of(n * slots, 16), slots)
            pre, up, hgrad = g.bg[part], g.bu[part], g.bh[part]
            sig = jax.nn.sigmoid(pre)
            silu = pre * sig
            act = (silu * up).astype(BF16).astype(F32)
            sens = jnp.sum(act * hgrad, axis=1, keepdims=True)
            g.gg[part] = (hgrad * up * sig * (1.0 + pre * (1.0 - sig))).astype(BF16)
            g.ug[part] = (hgrad * silu).astype(BF16)
            g.seall[part] = jnp.broadcast_to(sens, (slots, 128))
        g.sep[...] = g.seall[line_rows:]
        sens_d().start()

    def sens_out():
        sens_d().sent()
        sens_d().recv()
        g.sex[...] = g.seall[0:line_rows] + g.ser[...]
        for d in (1, 2, 3):
            sens_x(d).start()
        g.sei[0:slots] = g.sex[0:slots]

    def sens_combine(hits):
        block = g.sei.at[far]
        Move(block, block, g.sx_s.at[0], g.sx_r.at[0], mate).recv()
        found = [
            jnp.dot(hit, g.sei[...], precision=lax.Precision.HIGHEST, preferred_element_type=F32)
            for hit in hits
        ]
        lane = iota((2 * rows, 128), 1)
        both = jnp.where(lane == 0, found[0], jnp.where(lane == 1, found[1], 0.0))
        g.seown[...] = both[0:rows]
        g.seys[...] = both[rows:]
        sens_y().start()

    def sens_sent():
        block = g.sex.at[far]
        Move(block, block, g.sx_s.at[0], g.sx_r.at[0], mate).sent()
        sens_y().sent()

    def backward_finish(tick):
        sens_y().recv()
        sens = g.seown[...] + g.seyr[...]
        store = g.gan.at[tick]
        aff = [store[0:rows, k:k + 1] for k in range(2)]
        total = aff[0] + aff[1]
        weighted = aff[0] * sens[:, 0:1] + aff[1] * sens[:, 1:2]
        column = 4 + 2 * tick
        ids = g.idb[0:rows]
        experts = iota((rows, 8), 1)
        spread = jnp.zeros((rows, 8), F32)
        for k in range(2):
            lgrad = ROUTE_SCALE / total * (sens[:, k:k + 1] - weighted / total) * aff[k] * (1.0 - aff[k])
            spread = spread + jnp.where(ids[:, column + k:column + k + 1] == experts, lgrad, 0.0)
        high = spread.astype(BF16)
        rest = spread - high.astype(F32)
        mid = rest.astype(BF16)
        low = (rest - mid.astype(F32)).astype(BF16)

        def gather(ch, inner_sum):
            router = g.brouter[:, cols(ch)]
            y2_move(1, ch).recv()
            ngrad = g.owg[ch] + g.yrg[ch].astype(F32)
            ngrad = ngrad + (dot(high, router) + dot(mid, router) + dot(low, router))
            scaled = g.bgain[:, cols(ch)] * ngrad
            g.owg[ch] = scaled
            return inner_sum + jnp.sum(g.xs[tick, ch].astype(F32) * scaled, axis=1, keepdims=True)

        inner_sum = lax.fori_loop(0, nc, gather, jnp.zeros((rows, 1), F32))
        inv_rms = g.rsn[tick][:, 0:1]
        factor = inv_rms * inv_rms * inv_rms * (inner_sum / width)

        def body(ch):
            value = g.xc[tick, ch, 0:rows].astype(F32) + inv_rms * g.owg[ch]
            value = value - g.xs[tick, ch].astype(F32) * factor
            g.ob[tick, ch] = value.astype(BF16)
            deliver(1, tick, ch)
        chunks(body)

    def clear(*sums):
        for ref in sums:
            ref[...] = jnp.zeros_like(ref)

    def norm_saved(tick):
        def store(ch, value):
            g.tn[tick, ch, 0:rows] = value
        inv_rms = norm_rows(lambda ch: g.xs[tick, ch], g.bgain, store)
        g.rsn[tick] = jnp.broadcast_to(inv_rms, (rows, 128))

    def norm_forward(block, base):
        def store(ch, value):
            g.tf[ch, base:base + rows] = value
        norm_rows(lambda ch: block[ch, base:base + rows], g.fgain, store)

    def gate_move(tick):
        store = g.gan.at[tick]
        return Move(store.at[own_rows], store.at[mate_rows], g.ga_s.at[tick], g.ga_r.at[tick], mate)

    def gate_saved(tick):
        gating(g.tn.at[tick, :, own_rows], g.brouter, 4 + 2 * tick, g.gan.at[tick, own_rows])
        gate_move(tick).start()

    load_wait(saved_0)
    norm_saved(0)
    placer_n = own_packer(4)
    load_wait(cot_0)
    pl.semaphore_wait(barrier, len(partners))
    id_move.start()
    chunks(lambda ch: y_move(1, ch).start(), start=HEAD)
    chunks(pack(1, g.tn.at[0, :, own_rows], placer_n), stop=HEAD)
    for copy in weights:
        copy.start()
    for copy in small[2:]:
        copy.wait()
    id_move.recv()
    g.idall[...] = jnp.maximum(g.ids[...], g.idtb[...])
    g.idb[...] = g.idall[...].T
    placer_b = packer(4)
    chunks(
        y_recv(1), lambda ch: y_move(3, ch - HEAD).start(), pack(1, g.tn.at[0], placer_b), start=HEAD,
    )
    load_wait(act_0)
    norm_forward(g.xf0, 0)
    chunks(y_recv(3), y_ahead(3, 0), pack(3, g.xc.at[0], placer_b), swap_out(1), stop=HEAD)
    chunks(y_recv(3), y_ahead(3, 0), pack(3, g.xc.at[0], placer_b), share(1), start=HEAD)
    clear(g.bh, g.bg, g.bu, g.ag, g.au)
    placer_f = packer(0)
    load_wait(saved_1)
    norm_saved(1)
    chunks(swap_in(1), stop=HEAD)
    load_bgate.wait()
    load_bup.wait()
    chunks(
        y_recv(0), y_ahead(0, 2), share(3), pack(0, g.tf, placer_f),
        gather_up(1, g.wbg, g.wbu, g.bg, g.bu),
    )
    for ch in range(AHEAD, nc):
        y_move(2, ch).start()
    load_bdown.wait()
    chunks(gather_grad)

    @pl.when(first)
    def _():
        load_wait(act_1)
        load_wait(cot_1)
        chunks(lambda ch: feed_move(1, ch).start())

    for tick in range(2):
        backward_act()
        chunks(half_out(1))
        sens_out()
        half_sent(1, (1 + tick, 3))
        chunks(half_own(1), share(0))
        if tick == 0:
            gate_saved(0)
            gate_saved(1)
            gating(g.tf, g.frouter, 0, g.gaf)
            load_fgate.wait()
            load_fup.wait()
        chunks(gather_up(0, g.wfg, g.wfu, g.ag, g.au))
        activate()
        if tick == 0:
            load_fdown.wait()
        chunks(half_out(0))
        gate_move(tick).recv()
        mix, hit0, hit1 = mix_of(g.gan.at[tick], 4 + 2 * tick)
        sens_combine((hit0, hit1))
        half_sent(0, (0,))
        chunks(combine(1, mix), half_own(0))
        backward_finish(tick)
        mix, _, _ = mix_of(g.gaf, 2 * tick)
        if tick == 1:
            chunks(combine(0, mix))
            forward_finish(1)
            break
        placer_b = packer(6)
        packed_sent(1)
        clear(g.bh, g.bg, g.bu, g.ag, g.au)
        chunks(combine(0, mix), y_recv(2), pack(2, g.tn.at[1], placer_b))
        forward_finish(0)
        packed_sent(3)
        packed_sent(0)
        return_sent(0)
        return_sent(1)
        y_sent(0)
        sens_sent()
        chunks(arrived(1), pack(3, g.xc.at[1], placer_b), share(2))
        chunks(gather_up(2, g.wbg, g.wbu, g.bg, g.bu))
        chunks(arrived(0))
        norm_forward(g.xf1, 0)

        @pl.when(even)
        def _():
            chunks(lambda ch: y_move(0, ch).start())

        @pl.when(odd)
        def _():
            norm_forward(g.xf1, rows)

        placer_f = packer(2)
        chunks(lambda ch: pl.when(even)(y_move(0, ch).recv), pack(0, g.tf, placer_f), share(3))
        gating(g.tf, g.frouter, 2, g.gaf)
        chunks(gather_grad)

    for p in (0, 2, 3):
        packed_sent(p)
    for p in (1, 2, 3):
        y_sent(p)
    z_sent()
    for tick in range(2):
        gate_move(tick).sent()
    return_sent(0)
    return_sent(1)
    sens_sent()
    id_move.sent()

    def hop_sent(q, other):
        block = results[q].at[0]
        Move(block, block, g.hop_s.at[q, other], g.hop_r.at[q, other, 0], mate).sent()

    @pl.when(sender)
    def _():
        hop_sent(0, 0)
        hop_sent(1, 0)
        hop_sent(1, 1)

    @pl.when(sender & even)
    def _():
        hop_sent(0, 1)

    @pl.when(even)
    def _():
        y_sent(0)

    @pl.when(first)
    def _():
        block = inboxes[1].at[:, own_rows]
        Move(block, block, g.fy_s.at[1], g.hop_r.at[1, 1, 0], mate).sent()

    for q in range(2):
        pltpu.make_async_copy(results[q], results[q], g.ld_out.at[q]).wait()


def copy_kernel(a, b, out_a, out_b, held, sems):
    half = a.shape[1] // 2
    moves = [
        (src.at[tick, pl.ds(n * half, half)], held.at[2 * k + tick, pl.ds(n * half, half)],
         dst.at[tick, pl.ds(n * half, half)], 4 * k + 2 * tick + n)
        for k, (src, dst) in enumerate(((a, out_a), (b, out_b))) for tick in range(2) for n in range(2)
    ]
    into = [pltpu.make_async_copy(src, slot, sems.at[0, n]) for src, slot, dst, n in moves]
    back = [pltpu.make_async_copy(slot, dst, sems.at[1, n]) for src, slot, dst, n in moves]
    for copy in into:
        copy.start()
    for first_leg, second_leg in zip(into, back):
        first_leg.wait()
        second_leg.start()
    for copy in back:
        copy.wait()


def per_device(
    act_in, grad_in, feed, loss_grad, saved,
    fwd_gain, fwd_router, fwd_gate, fwd_up, fwd_down,
    bwd_gain, bwd_router, bwd_gate, bwd_up, bwd_down,
    fwd_routes, bwd_routes,
):
    rows, width = act_in.shape[1:]
    hid = fwd_gate.shape[2]
    experts = fwd_router.shape[2]
    cap = rows * fwd_routes.shape[3] // experts + rows // 8
    sections = lax.axis_size("section")
    nc = CHUNKS
    cw = width // nc
    slots = 2 * cap
    line = LINE * slots

    ids = jnp.concatenate([fwd_routes[0], bwd_routes[0]]).transpose(0, 2, 1).reshape(8, rows)
    ids = jnp.pad(ids, ((0, 0), (0, rows)), constant_values=-1)

    any_spec = pl.BlockSpec(memory_space=pl.ANY)

    def b(*shape):
        return pltpu.VMEM(shape, BF16)

    def f(*shape):
        return pltpu.VMEM(shape, F32)

    def i(*shape):
        return pltpu.VMEM(shape, jnp.int32)

    def dma(*shape):
        return pltpu.SemaphoreType.DMA(shape)

    scratch = [
        b(nc, rows, cw), b(nc, 2 * rows, cw), b(2, nc, 2 * rows, cw), b(2, nc, rows, cw),
        b(nc, 2 * rows, cw), b(2, nc, 2 * rows, cw),
        b(nc, 3 * slots, cw), b(nc, 3 * slots, cw), b(nc, 3 * slots, cw),
        b(nc, 2 * line, cw), b(nc, 2 * line, cw), b(nc, 2 * line, cw),
        b(nc, line, cw), b(nc, line, cw), b(nc, line, cw), b(nc, line, cw),
        b(nc, line, cw), b(nc, line, cw),
        b(nc, rows, cw), b(nc, rows, cw), b(nc, rows, cw), b(nc, rows, cw),
        f(nc, rows, cw), f(nc, rows, cw),
        b(2, nc, rows, cw), b(2, nc, rows, cw),
        b(width, hid), b(width, hid), b(hid, width),
        b(width, hid), b(width, hid), b(hid, width),
        f(2 * line, hid), f(2 * line, hid), f(2 * line, hid), f(2 * line, hid), f(2 * line, hid),
        b(2 * line, hid), b(2 * line, hid), b(2 * line, hid),
        f(2 * line, 128),
        f(line, 128), f(line, 128), f(line, 128), f(line, 128),
        f(rows, 128), f(rows, 128), f(rows, 128),
        f(2 * rows, 128), f(2, 2 * rows, 128), f(2, rows, 128),
        f(1, width), f(1, width), b(8, width), b(8, width), i(8, 2 * rows),
        b(HEAD, line // 2, cw), b(HEAD, line // 2, cw),
        i(2 * rows, 8), i(8, 2 * rows), i(8, 2 * rows), i(8, 2 * rows),
        dma(6), dma(6), dma(2),
        dma(4), dma(4, nc), dma(3), dma(3, nc), dma(3), dma(3, nc),
        dma(2), dma(2, nc), dma(2), dma(2, nc), dma(2), dma(2, nc),
        dma(2, 2), dma(2, 2, nc), dma(2),
        dma(1), dma(1), dma(1), dma(1), dma(1), dma(1), dma(1), dma(1), dma(2), dma(2), dma(1), dma(HEAD), dma(5),
    ]
    out_shape = jax.ShapeDtypeStruct((2, rows, width), BF16)
    call = pl.pallas_call(
        functools.partial(kernel, (rows, width, cap, hid, sections)),
        out_shape=(out_shape, out_shape),
        in_specs=[any_spec] * 16,
        out_specs=(any_spec, any_spec),
        scratch_shapes=scratch,
        compiler_params=pltpu.CompilerParams(
            collective_id=0, has_side_effects=True, vmem_limit_bytes=63 * 2**20
        ),
    )
    out_f, out_b = call(
        act_in[0], grad_in[0], feed[0], loss_grad[0], saved[0],
        fwd_gain, bwd_gain, fwd_router[0].T, bwd_router[0].T,
        fwd_gate[0], fwd_up[0], fwd_down[0], bwd_gate[0], bwd_up[0], bwd_down[0],
        ids,
    )
    out_f, out_b = pl.pallas_call(
        copy_kernel,
        out_shape=(out_shape, out_shape),
        in_specs=[any_spec] * 2,
        out_specs=(any_spec, any_spec),
        scratch_shapes=[b(4, rows, width), dma(2, 8)],
    )(out_f, out_b)
    return out_f[None], out_b[None]


def solution(mesh):
    in_specs = (
        P("section", "expert", None),
        P("section", "expert", None),
        P(None, "expert", None),
        P(None, "expert", None),
        P("section", None, "expert", None),
        P("section", None),
        P("section", None, None),
        P("section", None, "expert"),
        P("section", None, "expert"),
        P("section", "expert", None),
        P("section", None),
        P("section", None, None),
        P("section", None, "expert"),
        P("section", None, "expert"),
        P("section", "expert", None),
        P("section", None, "expert", None),
        P("section", None, "expert", None),
    )
    out_specs = (P("section", None, "expert", None), P("section", None, "expert", None))
    return jax.shard_map(
        per_device, mesh=mesh, in_specs=in_specs, out_specs=out_specs, check_vma=False
    )
```
